256 devices in a mesh: rows: 64 (over x, z_hi, y), grp: 4 (over z_lo, core).
Axes of the slice: x: 4, y: 4, z: 8 (z_hi: 4, z_lo: 2; z = z_hi * 2 + z_lo), core: 2. Of those that a mesh axis runs over, the one named last changes fastest.
Arguments:
- single: bfloat16 [768, 384], P('grp'), may hold values from -6 to 6
- pair: bfloat16 [768, 768, 128], P('rows', 'grp'), may hold values from -6 to 6
- chains: int32 [768], replicated, may hold values from 0 to 3, as said below
- noised: bfloat16 [64, 768, 768], P('rows', 'grp'), may hold values from -6 to 6
- w_gamma: bfloat16 [384, 768], replicated, may hold values from -0.3125 to 0.3125
- w_beta: bfloat16 [384, 768], replicated, may hold values from -0.3125 to 0.3125
- w_outgate: bfloat16 [384, 768], replicated, may hold values from -0.3125 to 0.3125
- w_query: bfloat16 [768, 768], replicated, may hold values from -0.21875 to 0.21875
- w_key: bfloat16 [768, 768], replicated, may hold values from -0.21875 to 0.21875
- w_value: bfloat16 [768, 768], replicated, may hold values from -0.21875 to 0.21875
- w_out: bfloat16 [768, 768], replicated, may hold values from -0.21875 to 0.21875
- w_pair: bfloat16 [128, 16], replicated, may hold values from -0.5 to 0.5
- chain_gain: float32 [16], replicated, may hold values from -3 to 6
- cotangent: bfloat16 [64, 768, 768], P('rows', 'grp'), may hold values from -6 to 6
Outputs:
- updated: bfloat16 [64, 768, 768], P('rows', 'grp')
- d_single: float32 [768, 384], P('grp')
- d_pair: bfloat16 [768, 768, 128], P('rows', 'grp')
The draws below stay inside these ranges and needn't reach their ends.
Inputs may be any that keep to these rules, and one draw needn't show every extreme that they name: `chains`: chain numbers never fall along the tokens; each chain has 1 to 384 tokens, one exactly 384.
All inputs are finite; a program needn't handle non-finite values.
Results may differ from the reference program's by a relative error of at most 0.022.
Values may be sent and summed in bfloat16 or wider, within the bound.
A program may use at most 128 MiB of HBM per device.

```python
import math
import jax
import jax.numpy as jnp
from jax import lax

D = 768
HEADS = 16
CS = 384
CZ = 128
TOKENS = 768
SAMPLES = 64


def chain_numbers(key):
    half_count = TOKENS // 2
    key_first, key_second, key_place = jax.random.split(key, 3)
    first_cut = jax.random.randint(key_first, (), 1, half_count - 1)
    second_cut = jax.random.randint(key_second, (), first_cut + 1, half_count)
    small_lengths = jnp.stack([first_cut, second_cut - first_cut, half_count - second_cut]).astype(jnp.int32)
    big_slot = jax.random.randint(key_place, (), 0, 4)
    slot_index = jnp.arange(4, dtype=jnp.int32)
    pick_index = jnp.clip(jnp.where(slot_index > big_slot, slot_index - 1, slot_index), 0, 2)
    lengths = jnp.where(slot_index == big_slot, half_count, jnp.take(small_lengths, pick_index)).astype(jnp.int32)
    chain_ends = jnp.cumsum(lengths).astype(jnp.int32)
    positions = jnp.arange(TOKENS, dtype=jnp.int32)
    return jnp.sum((positions[:, None] >= chain_ends[None, :3]).astype(jnp.int32), axis=1).astype(jnp.int32)


def draw_chains(key, part):
    numbers = chain_numbers(key)
    return numbers.astype(jnp.int32)


def draw_pair(key, part):
    key = jax.random.fold_in(key, 11)
    key_normal = jax.random.fold_in(key, 0)
    values = jax.random.normal(key_normal, (TOKENS, TOKENS, CZ), jnp.float32)
    return jnp.clip(values, -6.0, 6.0).astype(jnp.bfloat16)


def draw_chain_gain(key, part):
    key = jax.random.fold_in(key, 13)
    gains = jnp.clip(jax.random.normal(key, (HEADS,), jnp.float32), -3.0, 3.0)
    return gains.astype(jnp.float32)


def steps_of(stream_key, extent, cuts, least, high):
    level = 1.0
    for position, blocks in cuts:
        draws = jax.random.uniform(jax.random.fold_in(jax.random.fold_in(stream_key, 6), position), (blocks,), jnp.float32, least / len(cuts), high / len(cuts))
        level = level * jnp.repeat(jnp.exp(draws), extent[position] // blocks).reshape((-1,) + (1,) * (len(extent) - 1 - position))
    return level


def bell_draw(own_key, dims, width, bound, shards=(), kind=jnp.bfloat16):
    loudness = steps_of(own_key, dims, shards, -0.22, 0.18) if shards else 1.0
    drawn = jax.random.normal(own_key, dims, jnp.float32) * width * loudness
    return jnp.minimum(jnp.maximum(drawn, -bound), bound).astype(kind)


def setup_inputs(seed: int = 0) -> dict:
    splits = jax.random.split(jax.random.key(seed), 15)
    return {
        "single": bell_draw(splits[0], (TOKENS, CS), 1.0, 6.0, ((0, 4),)),
        "pair": draw_pair(jax.random.fold_in(splits[14], 71), 0),
        "chains": draw_chains(jax.random.fold_in(splits[14], 71), 0),
        "noised": bell_draw(splits[3], (SAMPLES, TOKENS, D), 1.0, 6.0, ((0, 64), (1, 4))),
        "w_gamma": bell_draw(splits[4], (CS, D), CS ** -0.5, 0.3125),
        "w_beta": bell_draw(splits[5], (CS, D), CS ** -0.5, 0.3125),
        "w_outgate": bell_draw(splits[6], (CS, D), CS ** -0.5, 0.3125),
        "w_query": bell_draw(splits[7], (D, D), D ** -0.5, 0.21875),
        "w_key": bell_draw(splits[8], (D, D), D ** -0.5, 0.21875),
        "w_value": bell_draw(splits[9], (D, D), D ** -0.5, 0.21875),
        "w_out": bell_draw(splits[10], (D, D), D ** -0.5, 0.21875),
        "w_pair": bell_draw(splits[11], (CZ, HEADS), CZ ** -0.5, 0.5),
        "chain_gain": draw_chain_gain(jax.random.fold_in(splits[14], 71), 0),
        "cotangent": bell_draw(splits[13], (SAMPLES, TOKENS, D), 1.0, 6.0, ((0, 64), (1, 4))),
    }


EPSILON = 1e-05

def norm_rows(values):
    center = values - lax.optimization_barrier(jnp.mean(values, axis=-1, keepdims=True))
    inverse = lax.rsqrt(lax.optimization_barrier(jnp.mean(center * center, axis=-1, keepdims=True)) + EPSILON)
    return (center * inverse, inverse)

def norm_back(grad_in, normed, inverse):
    grad_mean = lax.optimization_barrier(jnp.mean(grad_in, axis=-1, keepdims=True))
    cross_mean = lax.optimization_barrier(jnp.mean(grad_in * normed, axis=-1, keepdims=True))
    return inverse * (grad_in - grad_mean - normed * cross_mean)

def matmul(left, right):
    return jnp.dot(left, right, preferred_element_type=jnp.float32)

def reference(single, pair, chains, noised, w_gamma, w_beta, w_outgate, w_query, w_key, w_value, w_out, w_pair, chain_gain, cotangent):
    head_size = D // HEADS
    score_scale = 1.0 / math.sqrt(head_size)
    single_norm, single_inv = norm_rows(single.astype(jnp.float32))
    single_b = single_norm.astype(jnp.bfloat16)
    cond_gamma = jax.nn.sigmoid(matmul(single_b, w_gamma))
    cond_beta = matmul(single_b, w_beta)
    out_gate = jax.nn.sigmoid(matmul(single_b, w_outgate))

    def project_row(pair_row):
        normed, inverse_row = norm_rows(pair_row.astype(jnp.float32))
        return matmul(normed.astype(jnp.bfloat16), w_pair)
    projected = lax.map(project_row, pair)
    same_chain = (chains[:, None] == chains[None, :]).astype(jnp.float32)
    bias = (jnp.transpose(projected, (2, 0, 1)) + chain_gain[:, None, None] * same_chain[None]).astype(jnp.bfloat16)
    bias_f = bias.astype(jnp.float32)

    def sample_step(carry, inputs):
        bias_sum, gamma_sum, beta_sum, gate_sum = carry
        sample_in, sample_grad = inputs
        noised_f = sample_in.astype(jnp.float32)
        noised_norm, noised_inv = norm_rows(noised_f)
        x_b = (noised_norm * cond_gamma + cond_beta).astype(jnp.bfloat16)
        queries = matmul(x_b, w_query).astype(jnp.bfloat16)
        keys = matmul(x_b, w_key).astype(jnp.bfloat16)
        values = matmul(x_b, w_value).astype(jnp.bfloat16)
        query_heads = queries.reshape(TOKENS, HEADS, head_size).astype(jnp.float32)
        key_heads = keys.reshape(TOKENS, HEADS, head_size).astype(jnp.float32)
        value_heads = values.reshape(TOKENS, HEADS, head_size).astype(jnp.float32)
        scores = jnp.einsum('ihe,jhe->hij', query_heads, key_heads) * score_scale + bias_f
        exp_scores = jnp.exp(scores)
        attn_prob = exp_scores / lax.optimization_barrier(jnp.sum(exp_scores, axis=-1, keepdims=True))
        prob_b = attn_prob.astype(jnp.bfloat16)
        attended = jnp.einsum('hij,jhe->ihe', prob_b.astype(jnp.float32), value_heads).reshape(TOKENS, D).astype(jnp.bfloat16)
        block_update = matmul(attended, w_out)
        updated = (noised_f + out_gate * block_update).astype(jnp.bfloat16)
        grad_out = sample_grad.astype(jnp.float32)
        gate_part = grad_out * block_update
        grad_update = (grad_out * out_gate).astype(jnp.bfloat16)
        grad_attn = matmul(grad_update, w_out.T).astype(jnp.bfloat16)
        grad_heads = grad_attn.reshape(TOKENS, HEADS, head_size).astype(jnp.float32)
        grad_prob = jnp.einsum('ihe,jhe->hij', grad_heads, value_heads)
        row_delta = lax.optimization_barrier(jnp.sum(attn_prob * grad_prob, axis=-1, keepdims=True))
        grad_score = attn_prob * (grad_prob - row_delta)
        score_b = grad_score.astype(jnp.bfloat16).astype(jnp.float32)
        grad_query = (jnp.einsum('hij,jhe->ihe', score_b, key_heads) * score_scale).reshape(TOKENS, D).astype(jnp.bfloat16)
        grad_key = (jnp.einsum('hij,ihe->jhe', score_b, query_heads) * score_scale).reshape(TOKENS, D).astype(jnp.bfloat16)
        grad_value = jnp.einsum('hij,ihe->jhe', prob_b.astype(jnp.float32), grad_heads).reshape(TOKENS, D).astype(jnp.bfloat16)
        grad_input = matmul(grad_query, w_query.T) + matmul(grad_key, w_key.T) + matmul(grad_value, w_value.T)
        new_carry = (bias_sum + score_b, gamma_sum + grad_input * noised_norm, beta_sum + grad_input, gate_sum + gate_part)
        return (new_carry, updated)
    start = (jnp.zeros((HEADS, TOKENS, TOKENS), jnp.float32), jnp.zeros((TOKENS, D), jnp.float32), jnp.zeros((TOKENS, D), jnp.float32), jnp.zeros((TOKENS, D), jnp.float32))
    finals, updated = lax.scan(sample_step, start, (noised, cotangent))
    bias_sum, gamma_sum, beta_sum, gate_sum = finals
    pre_gamma = (gamma_sum * cond_gamma * (1.0 - cond_gamma)).astype(jnp.bfloat16)
    pre_gate = (gate_sum * out_gate * (1.0 - out_gate)).astype(jnp.bfloat16)
    grad_snorm = matmul(pre_gamma, w_gamma.T) + matmul(beta_sum.astype(jnp.bfloat16), w_beta.T) + matmul(pre_gate, w_outgate.T)
    d_single = norm_back(grad_snorm, single_norm, single_inv)
    bias_grad = jnp.transpose((bias_sum * TOKENS).astype(jnp.bfloat16), (1, 2, 0))

    def pair_row_back(inputs):
        pair_row, grad_row = inputs
        normed, inverse_row = norm_rows(pair_row.astype(jnp.float32))
        grad_pairn = matmul(grad_row, w_pair.T)
        return norm_back(grad_pairn, normed, inverse_row).astype(jnp.bfloat16)
    d_pair = lax.map(pair_row_back, (pair, bias_grad))
    return (updated, d_single, d_pair)
```

```python
import math

import jax
import jax.numpy as jnp
from jax import lax
from jax.experimental import pallas as pl
from jax.experimental.pallas import tpu as pltpu
from jax.sharding import PartitionSpec as P

EPSILON = 1e-05
LOG2E = math.log2(math.e)
F32 = jnp.float32
BF16 = jnp.bfloat16
MESH = pl.DeviceIdType.MESH
ANY = pl.BlockSpec(memory_space=pl.ANY)
VMEM = pl.BlockSpec(memory_space=pltpu.VMEM)
SMEM = pl.BlockSpec(memory_space=pltpu.SMEM)
VMEM_BYTES = 56 * 1024 * 1024

HEADS = 16
HEAD = 48
WIDTH = 768
TOKENS = 768
BLOCK = 192
ROWS = 12
CHUNK = 6 * HEAD


def dot(left, right, contract=((1,), (0,))):
    return lax.dot_general(left, right, (contract, ((), ())), preferred_element_type=F32)


def norm_rows(values):
    center = values - jnp.mean(values, axis=-1, keepdims=True)
    inverse = lax.rsqrt(jnp.mean(center * center, axis=-1, keepdims=True) + EPSILON)
    return center * inverse, inverse


def norm_back(grad_in, normed, inverse):
    grad_mean = jnp.mean(grad_in, axis=-1, keepdims=True)
    cross_mean = jnp.mean(grad_in * normed, axis=-1, keepdims=True)
    return inverse * (grad_in - grad_mean - normed * cross_mean)


def iota(shape, dim):
    return lax.broadcasted_iota(jnp.int32, shape, dim)


def front_kernel(
    single,
    pair,
    chain_all,
    chain_cols,
    noised,
    w_gamma,
    w_beta,
    w_outgate,
    w_query,
    w_key,
    w_value,
    w_out,
    w_pair,
    chain_gain,
    cotangent,
    bias_out,
    acts_out,
    gamma_out,
    gate_out,
):
    row_index = lax.axis_index("rows")
    group_index = lax.axis_index("grp")
    cols = chain_cols[pl.ds(group_index, 1), :]
    w_pair_t = w_pair[...].astype(F32).T.astype(BF16)
    gain = chain_gain[...]
    strips = []
    for i in range(ROWS):
        normed, _ = norm_rows(pair[i].astype(F32))
        projected = dot(w_pair_t, normed.astype(BF16), ((1,), (1,)))
        same = (cols == chain_all[row_index * ROWS + i]).astype(F32)
        strips.append((projected + gain * same).astype(BF16))
    strips = jnp.concatenate(strips, axis=0)
    shape = (HEADS * 16, HEADS * ROWS)
    to, source = iota(shape, 0), iota(shape, 1)
    order = ((to // 16 == source % 16) & (to % 16 == source // 16)).astype(BF16)
    bias_out[:, :BLOCK] = dot(order, strips).astype(BF16)
    bias_out[:, BLOCK:] = jnp.zeros((HEADS * 16, 256 - BLOCK), BF16)

    single_norm, _ = norm_rows(single[...].astype(F32))
    single_b = single_norm.astype(BF16)
    gamma = jax.nn.sigmoid(dot(single_b, w_gamma[...]))
    beta = dot(single_b, w_beta[...])
    gate = jax.nn.sigmoid(dot(single_b, w_outgate[...]))
    gamma_out[...] = gamma
    gate_out[...] = gate
    noised_norm, _ = norm_rows(noised[...].astype(F32))
    x_b = (noised_norm * gamma + beta).astype(BF16)
    grad_update = (cotangent[...].astype(F32) * gate).astype(BF16)
    arrays = [
        dot(x_b, w_query[...]),
        dot(x_b, w_key[...]),
        dot(x_b, w_value[...]),
        dot(grad_update, w_out[...], ((1,), (1,))),
    ]
    pieces = [a[:128].T.astype(BF16) for a in arrays]
    for first, second in ((0, 2), (1, 3)):
        tail = jnp.concatenate([arrays[first][128:], arrays[second][128:]], axis=0)
        pieces.append(tail.T.astype(BF16))
    for h in range(HEADS):
        for n, piece in enumerate(pieces):
            acts_out[h * CHUNK + n * HEAD : h * CHUNK + (n + 1) * HEAD, :] = piece[
                h * HEAD : (h + 1) * HEAD
            ]


class Place:
    def __init__(self):
        self.r = lax.axis_index("rows")
        self.b = lax.axis_index("grp")
        self.x = self.r // 16
        self.z = (self.r // 4) % 4
        self.y = self.r % 4
        self.me = self.y * 4 + self.b

    def group(self, k):
        peer = (self.me + k) % 16
        return peer, (self.r - self.y + peer // 4, peer % 4)

    def group_from(self, k):
        return (self.me + 16 - k) % 16

    def along(self, axis, k):
        if axis == "x":
            place = (self.x + k) % 4
            return place, (self.r + (place - self.x) * 16, self.b)
        if axis == "z":
            place = (self.z + k) % 4
            return place, (self.r + (place - self.z) * 4, self.b)
        place = (self.y + k) % 4
        return place, (self.r + (place - self.y), self.b)

    def along_from(self, axis, k):
        return ({"x": self.x, "z": self.z, "y": self.y}[axis] + 4 - k) % 4


def remote(source, target, send, recv, device):
    return pltpu.make_async_remote_copy(
        src_ref=source,
        dst_ref=target,
        send_sem=send,
        recv_sem=recv,
        device_id=device,
        device_id_type=MESH,
    )


def enter(devices):
    barrier = pltpu.get_barrier_semaphore()
    for device in devices:
        pl.semaphore_signal(barrier, inc=1, device_id=device, device_id_type=MESH)
    pl.semaphore_wait(barrier, len(devices))


def gather_kernel(
    bias_in, acts_in, acts_all, bias_all, held, mine, a_send, a_recv, b_send, b_recv, s_send, s_recv, local
):
    at = Place()
    enter(
        [at.group(k)[1] for k in range(1, 16)]
        + [at.along("z", k)[1] for k in range(1, 4)]
        + [at.along("x", k)[1] for k in range(1, 4)]
    )
    out = []
    for k in range(1, 16):
        peer, device = at.group(k)
        copy = remote(bias_in.at[peer], held.at[at.me], b_send.at[k], b_recv.at[k], device)
        copy.start()
        out.append(copy)
    own_bias = pltpu.make_async_copy(bias_in.at[at.me], held.at[at.me], local.at[0])
    own_bias.start()
    for k in range(1, 16):
        peer, device = at.group(k)
        copy = remote(acts_in.at[peer], acts_all.at[at.me], a_send.at[k], a_recv.at[k], device)
        copy.start()
        out.append(copy)
    own_acts = pltpu.make_async_copy(acts_in.at[at.me], acts_all.at[at.me], local.at[1])
    own_acts.start()

    own_bias.wait()
    for k in range(1, 16):
        source = at.group_from(k)
        remote(
            bias_in.at[source], held.at[source], b_send.at[k], b_recv.at[k], at.group(k)[1]
        ).wait_recv()
    strips = []
    for y in range(4):
        parts = [held[y * 4 + b] for b in range(4)]
        tails = [p[:, 128:BLOCK] for p in parts]
        strips.append(jnp.concatenate([p[:, :128] for p in parts] + tails, axis=1))
    strips = jnp.concatenate(strips, axis=0)
    to, source = iota((HEAD, 64), 0), iota((HEAD, 64), 1)
    pick = ((source // 16 == to // ROWS) & (source % 16 == to % ROWS)).astype(BF16)
    mine[...] = dot(pick, strips).astype(BF16)
    own_rows = pltpu.make_async_copy(mine, bias_all.at[at.x, at.z], local.at[2])
    own_rows.start()
    for k in range(1, 4):
        _, device = at.along("z", k)
        copy = remote(mine, bias_all.at[at.x, at.z], s_send.at[k], s_recv.at[k], device)
        copy.start()
        out.append(copy)
    own_rows.wait()
    for k in range(1, 4):
        source = at.along_from("z", k)
        remote(
            mine, bias_all.at[at.x, source], s_send.at[k], s_recv.at[k], at.along("z", k)[1]
        ).wait_recv()
    for k in range(1, 4):
        _, device = at.along("x", k)
        copy = remote(bias_all.at[at.x], bias_all.at[at.x], s_send.at[4 + k], s_recv.at[4 + k], device)
        copy.start()
        out.append(copy)
    for k in range(1, 4):
        source = at.along_from("x", k)
        remote(
            bias_all.at[source],
            bias_all.at[source],
            s_send.at[4 + k],
            s_recv.at[4 + k],
            at.along("x", k)[1],
        ).wait_recv()
    own_acts.wait()
    for k in range(1, 16):
        source = at.group_from(k)
        remote(
            acts_in.at[source], acts_all.at[source], a_send.at[k], a_recv.at[k], at.group(k)[1]
        ).wait_recv()
    for copy in out:
        copy.wait_send()


def scatter_kernel(
    grads_in, bias_in, grads_all, bias_out, from_x, to_z, from_z, to_group,
    a_send, a_recv, b_send, b_recv, s_send, s_recv, local,
):
    at = Place()
    enter(
        [at.group(k)[1] for k in range(1, 16)]
        + [at.along("z", k)[1] for k in range(1, 4)]
        + [at.along("x", k)[1] for k in range(1, 4)]
    )
    out = []
    for k in range(1, 4):
        place, device = at.along("x", k)
        copy = remote(bias_in.at[place], from_x.at[at.x], s_send.at[k], s_recv.at[k], device)
        copy.start()
        out.append(copy)
    own_bias = pltpu.make_async_copy(bias_in.at[at.x], from_x.at[at.x], local.at[0])
    own_bias.start()
    for k in range(1, 16):
        peer, device = at.group(k)
        copy = remote(grads_in.at[peer], grads_all.at[at.me], a_send.at[k], a_recv.at[k], device)
        copy.start()
        out.append(copy)
    own_acts = pltpu.make_async_copy(grads_in.at[at.me], grads_all.at[at.me], local.at[1])
    own_acts.start()

    own_bias.wait()
    for k in range(1, 4):
        source = at.along_from("x", k)
        remote(
            bias_in.at[source], from_x.at[source], s_send.at[k], s_recv.at[k], at.along("x", k)[1]
        ).wait_recv()
    for z in range(4):
        rows = slice(z * HEAD, (z + 1) * HEAD)
        total = from_x[0, rows, :].astype(F32)
        for x in range(1, 4):
            total = total + from_x[x, rows, :].astype(F32)
        to_z[z] = total.astype(BF16)
    for k in range(1, 4):
        place, device = at.along("z", k)
        copy = remote(to_z.at[place], from_z.at[at.z], s_send.at[4 + k], s_recv.at[4 + k], device)
        copy.start()
        out.append(copy)
    own_rows = pltpu.make_async_copy(to_z.at[at.z], from_z.at[at.z], local.at[2])
    own_rows.start()
    own_rows.wait()
    for k in range(1, 4):
        source = at.along_from("z", k)
        remote(
            to_z.at[source], from_z.at[source], s_send.at[4 + k], s_recv.at[4 + k], at.along("z", k)[1]
        ).wait_recv()
    total = from_z[0].astype(F32)
    for z in range(1, 4):
        total = total + from_z[z].astype(F32)
    total = (total * TOKENS).astype(BF16)
    to, source = iota((64, HEAD), 0), iota((64, HEAD), 1)
    pick = ((to // 16 == source // ROWS) & (to % 16 == source % ROWS)).astype(BF16)
    spread = dot(pick, total).astype(BF16)
    for y in range(4):
        rows = spread[y * 16 : (y + 1) * 16]
        for b in range(4):
            tail = rows[:, 512 + b * 64 : 512 + (b + 1) * 64]
            to_group[y * 4 + b, :, :128] = rows[:, b * 128 : (b + 1) * 128]
            to_group[y * 4 + b, :, 128:] = jnp.concatenate([tail, jnp.zeros_like(tail)], axis=1)
    for k in range(1, 16):
        peer, device = at.group(k)
        copy = remote(to_group.at[peer], bias_out.at[at.me], b_send.at[k], b_recv.at[k], device)
        copy.start()
        out.append(copy)
    own_group = pltpu.make_async_copy(to_group.at[at.me], bias_out.at[at.me], local.at[3])
    own_group.start()
    own_acts.wait()
    for k in range(1, 16):
        source = at.group_from(k)
        remote(
            grads_in.at[source], grads_all.at[source], a_send.at[k], a_recv.at[k], at.group(k)[1]
        ).wait_recv()
    own_group.wait()
    for k in range(1, 16):
        source = at.group_from(k)
        remote(
            to_group.at[source], bias_out.at[source], b_send.at[k], b_recv.at[k], at.group(k)[1]
        ).wait_recv()
    for copy in out:
        copy.wait_send()


def reduce_kernel(part, single, result, from_y, from_z, from_x, own, send, recv):
    at = Place()
    enter([at.along(axis, k)[1] for axis in "yzx" for k in range(1, 4)])
    out = []

    def exchange(first, source, target, slot, axis):
        for k in range(1, 4):
            place, device = at.along(axis, k)
            copy = remote(source(place), target(slot), send.at[first + k], recv.at[first + k], device)
            copy.start()
            out.append(copy)
        for k in range(1, 4):
            place = at.along_from(axis, k)
            remote(
                source(slot), target(place), send.at[first + k], recv.at[first + k], at.along(axis, k)[1]
            ).wait_recv()

    def total(ref):
        value = ref[0].astype(F32)
        for n in range(1, 4):
            value = value + ref[n].astype(F32)
        return value

    from_y[pl.ds(at.y, 1)] = part[pl.ds(at.y, 1)]
    exchange(0, lambda p: part.at[p], lambda p: from_y.at[p], at.y, "y")
    from_z[pl.ds(at.z, 1)] = total(from_y).astype(BF16)[None]
    exchange(4, lambda p: from_z.at[at.z], lambda p: from_z.at[p], at.z, "z")
    from_x[pl.ds(at.x, 1)] = total(from_z).astype(BF16)[None]
    exchange(8, lambda p: from_x.at[at.x], lambda p: from_x.at[p], at.x, "x")
    normed, inverse = norm_rows(single[pl.ds(at.y, 1)][0].astype(F32))
    final = norm_back(total(from_x), normed, inverse)
    own[...] = final
    result[pl.ds(at.y, 1)] = final[None]
    exchange(12, lambda p: own, lambda p: result.at[p], at.y, "y")
    for copy in out:
        copy.wait_send()


def attention_kernel(acts, bias, grads, bias_grad, total_grad):
    sample = pl.program_id(0)
    scale = 1.0 / math.sqrt(HEAD)

    @pl.when(sample == 0)
    def _():
        total_grad[...] = jnp.zeros_like(total_grad)

    def piece(b, n):
        return acts[0, b * CHUNK + n * HEAD : b * CHUNK + (n + 1) * HEAD, :]

    def wide(n, tail, half):
        lanes = slice(half * 64, half * 64 + 64)
        parts = [piece(b, n) for b in range(4)] + [piece(b, tail)[:, lanes] for b in range(4)]
        return jnp.concatenate(parts, axis=1)

    def block(b, n, tail, half):
        lanes = slice(half * 64, half * 64 + 64)
        return jnp.concatenate([piece(b, n), piece(b, tail)[:, lanes]], axis=1)

    key_t = wide(1, 5, 0)
    value_t = wide(2, 4, 1)
    grad_key = jnp.zeros((HEAD, TOKENS), F32)
    grad_value = jnp.zeros((HEAD, TOKENS), F32)
    for b in range(4):
        rows = slice(b * BLOCK, (b + 1) * BLOCK)
        query_t = block(b, 0, 4, 0)
        grad_t = block(b, 3, 5, 1)
        query = query_t.astype(F32).T.astype(BF16)
        grad = grad_t.astype(F32).T.astype(BF16)
        scores = dot(query, key_t) * (scale * LOG2E) + bias[rows, :].astype(F32) * LOG2E
        weight = jnp.exp2(scores)
        prob = weight * (1.0 / jnp.sum(weight, axis=-1, keepdims=True))
        prob_b = prob.astype(BF16)
        grad_prob = dot(grad, value_t)
        scaled = prob * grad_prob
        grad_score = scaled - prob * jnp.sum(scaled, axis=-1, keepdims=True)
        score_b = grad_score.astype(BF16)
        total_grad[rows, :] = total_grad[rows, :] + grad_score
        attended = dot(value_t, prob_b, ((1,), (1,))).astype(BF16)
        grad_query = (dot(key_t, score_b, ((1,), (1,))) * scale).astype(BF16)
        grad_value = grad_value + dot(grad_t, prob_b)
        grad_key = grad_key + dot(query_t, score_b)
        first = b * CHUNK
        grads[0, first : first + HEAD, :] = attended[:, :128]
        grads[0, first + HEAD : first + 2 * HEAD, :] = grad_query[:, :128]
        grads[0, first + 4 * HEAD : first + 5 * HEAD, :64] = attended[:, 128:]
        grads[0, first + 5 * HEAD : first + 6 * HEAD, :64] = grad_query[:, 128:]
    grad_key = (grad_key * scale).astype(BF16)
    grad_value = grad_value.astype(BF16)
    for b in range(4):
        first = b * CHUNK
        lanes = slice(b * 128, (b + 1) * 128)
        tail = slice(512 + b * 64, 512 + (b + 1) * 64)
        grads[0, first + 2 * HEAD : first + 3 * HEAD, :] = grad_key[:, lanes]
        grads[0, first + 3 * HEAD : first + 4 * HEAD, :] = grad_value[:, lanes]
        grads[0, first + 4 * HEAD : first + 5 * HEAD, 64:] = grad_key[:, tail]
        grads[0, first + 5 * HEAD : first + 6 * HEAD, 64:] = grad_value[:, tail]

    @pl.when(sample == 3)
    def _():
        bias_grad[...] = total_grad[...].astype(BF16)


def back_kernel(
    grads, noised, cotangent, gamma_in, gate_in,
    w_gamma, w_beta, w_outgate, w_query, w_key, w_value, w_out,
    updated, part,
):
    def piece(n):
        rows = [grads[h * CHUNK + n * HEAD : h * CHUNK + (n + 1) * HEAD, :] for h in range(HEADS)]
        return jnp.concatenate(rows, axis=0).astype(F32).T.astype(BF16)

    tails = [piece(4), piece(5)]
    attended = jnp.concatenate([piece(0), tails[0][:64]], axis=0)
    grad_query = jnp.concatenate([piece(1), tails[1][:64]], axis=0)
    grad_key = jnp.concatenate([piece(2), tails[0][64:]], axis=0)
    grad_value = jnp.concatenate([piece(3), tails[1][64:]], axis=0)
    gamma = gamma_in[...]
    gate = gate_in[...]
    block_update = dot(attended, w_out[...])
    noised_f = noised[...].astype(F32)
    updated[...] = (noised_f + gate * block_update).astype(BF16)
    noised_norm, _ = norm_rows(noised_f)
    back = ((1,), (1,))
    grad_input = (
        dot(grad_query, w_query[...], back)
        + dot(grad_key, w_key[...], back)
        + dot(grad_value, w_value[...], back)
    )
    pre_gamma = (grad_input * noised_norm * (gamma * (1.0 - gamma))).astype(BF16)
    pre_gate = (cotangent[...].astype(F32) * block_update * (gate * (1.0 - gate))).astype(BF16)
    total = dot(pre_gamma, w_gamma[...], back)
    total = total + dot(grad_input.astype(BF16), w_beta[...], back)
    total = total + dot(pre_gate, w_outgate[...], back)
    part[...] = total.astype(BF16)


def pair_kernel(bias_grad, pair, w_pair, result):
    grad_t = bias_grad[...].astype(F32).T.astype(BF16)[:BLOCK]
    shape = (HEADS * 16, HEADS)
    pick = (iota(shape, 0) // 16 == iota(shape, 1)).astype(BF16)
    weight = dot(pick, w_pair[...], ((1,), (1,))).astype(BF16)
    row = iota(weight.shape, 0) % 16
    for i in range(ROWS):
        grad = dot(grad_t, jnp.where(row == i, weight, jnp.zeros_like(weight)))
        normed, inverse = norm_rows(pair[i].astype(F32))
        result[i] = norm_back(grad, normed, inverse).astype(BF16)


def on_device(
    single,
    pair,
    chains,
    noised,
    w_gamma,
    w_beta,
    w_outgate,
    w_query,
    w_key,
    w_value,
    w_out,
    w_pair,
    chain_gain,
    cotangent,
):
    noised = noised.reshape(BLOCK, WIDTH)
    cotangent = cotangent.reshape(BLOCK, WIDTH)
    local = pltpu.CompilerParams(vmem_limit_bytes=VMEM_BYTES)

    def sends(collective):
        return pltpu.CompilerParams(
            vmem_limit_bytes=VMEM_BYTES, collective_id=collective, has_side_effects=True
        )

    bias_send, acts_send, gamma, gate = pl.pallas_call(
        front_kernel,
        out_shape=[
            jax.ShapeDtypeStruct((HEADS * 16, 256), BF16),
            jax.ShapeDtypeStruct((HEADS * CHUNK, 128), BF16),
            jax.ShapeDtypeStruct((BLOCK, WIDTH), F32),
            jax.ShapeDtypeStruct((BLOCK, WIDTH), F32),
        ],
        in_specs=[VMEM, VMEM, SMEM] + [VMEM] * 12,
        out_specs=[VMEM] * 4,
        compiler_params=local,
        name="front",
    )(
        single,
        pair,
        chains,
        chains.reshape(4, BLOCK),
        noised,
        w_gamma,
        w_beta,
        w_outgate,
        w_query,
        w_key,
        w_value,
        w_out,
        w_pair,
        chain_gain.reshape(HEADS, 1),
        cotangent,
    )
    dma = pltpu.SemaphoreType.DMA
    acts_all, bias_all = pl.pallas_call(
        gather_kernel,
        out_shape=[
            jax.ShapeDtypeStruct((16, CHUNK, 128), BF16),
            jax.ShapeDtypeStruct((4, 4, HEAD, TOKENS), BF16),
        ],
        in_specs=[ANY, ANY],
        out_specs=[ANY, ANY],
        scratch_shapes=[
            pltpu.VMEM((16, 16, 256), BF16),
            pltpu.VMEM((HEAD, TOKENS), BF16),
            dma((16,)),
            dma((16,)),
            dma((16,)),
            dma((16,)),
            dma((8,)),
            dma((8,)),
            dma((3,)),
        ],
        compiler_params=sends(0),
        name="gather",
    )(bias_send.reshape(HEADS, 16, 256), acts_send.reshape(HEADS, CHUNK, 128))
    grads, bias_grad = pl.pallas_call(
        attention_kernel,
        grid=(4,),
        out_shape=[
            jax.ShapeDtypeStruct((4, 4 * CHUNK, 128), BF16),
            jax.ShapeDtypeStruct((TOKENS, TOKENS), BF16),
        ],
        in_specs=[
            pl.BlockSpec((1, 4 * CHUNK, 128), lambda s: (s, 0, 0)),
            pl.BlockSpec((TOKENS, TOKENS), lambda s: (0, 0)),
        ],
        out_specs=[
            pl.BlockSpec((1, 4 * CHUNK, 128), lambda s: (s, 0, 0)),
            pl.BlockSpec((TOKENS, TOKENS), lambda s: (0, 0)),
        ],
        scratch_shapes=[pltpu.VMEM((TOKENS, TOKENS), F32)],
        compiler_params=local,
        name="attention",
    )(acts_all.reshape(4, 4 * CHUNK, 128), bias_all.reshape(TOKENS, TOKENS))
    grads_all, bias_own = pl.pallas_call(
        scatter_kernel,
        out_shape=[
            jax.ShapeDtypeStruct((16, CHUNK, 128), BF16),
            jax.ShapeDtypeStruct((16, 16, 256), BF16),
        ],
        in_specs=[ANY, ANY],
        out_specs=[ANY, ANY],
        scratch_shapes=[
            pltpu.VMEM((4, BLOCK, TOKENS), BF16),
            pltpu.VMEM((4, HEAD, TOKENS), BF16),
            pltpu.VMEM((4, HEAD, TOKENS), BF16),
            pltpu.VMEM((16, 16, 256), BF16),
            dma((16,)),
            dma((16,)),
            dma((16,)),
            dma((16,)),
            dma((8,)),
            dma((8,)),
            dma((4,)),
        ],
        compiler_params=sends(1),
        name="scatter",
    )(grads.reshape(16, CHUNK, 128), bias_grad.reshape(4, BLOCK, TOKENS))
    updated, part = pl.pallas_call(
        back_kernel,
        out_shape=[
            jax.ShapeDtypeStruct((BLOCK, WIDTH), BF16),
            jax.ShapeDtypeStruct((BLOCK, WIDTH // 2), BF16),
        ],
        in_specs=[VMEM] * 12,
        out_specs=[VMEM] * 2,
        compiler_params=local,
        name="back",
    )(
        grads_all.reshape(16 * CHUNK, 128),
        noised,
        cotangent,
        gamma,
        gate,
        w_gamma,
        w_beta,
        w_outgate,
        w_query,
        w_key,
        w_value,
        w_out,
    )
    quarter = (4, HEAD, WIDTH // 2)
    d_single = pl.pallas_call(
        reduce_kernel,
        out_shape=jax.ShapeDtypeStruct(quarter, F32),
        in_specs=[VMEM] * 2,
        out_specs=VMEM,
        scratch_shapes=[pltpu.VMEM(quarter, BF16)] * 3
        + [pltpu.VMEM(quarter[1:], F32), dma((16,)), dma((16,))],
        compiler_params=sends(2),
        name="reduce",
    )(part.reshape(quarter), single.reshape(quarter))
    d_pair = pl.pallas_call(
        pair_kernel,
        out_shape=jax.ShapeDtypeStruct(pair.shape, BF16),
        in_specs=[VMEM] * 3,
        out_specs=VMEM,
        compiler_params=local,
        name="pair",
    )(bias_own.reshape(256, 256), pair, w_pair)
    return (
        updated.reshape(1, BLOCK, WIDTH),
        d_single.reshape(BLOCK, WIDTH // 2),
        d_pair,
    )


def solution(mesh):
    rows = P("rows", "grp", None)
    grp = P("grp", None)
    in_specs = (grp, rows, P(), rows) + (P(),) * 9 + (rows,)
    return jax.shard_map(
        on_device, mesh=mesh, in_specs=in_specs, out_specs=(rows, grp, rows), check_vma=False
    )
```

```python
import math

import jax
import jax.numpy as jnp
from jax import lax
from jax.experimental import pallas as pl
from jax.experimental.pallas import tpu as pltpu
from jax.sharding import PartitionSpec as P

EPSILON = 1e-05
LOG2E = math.log2(math.e)
F32 = jnp.float32
BF16 = jnp.bfloat16
MESH = pl.DeviceIdType.MESH
ANY = pl.BlockSpec(memory_space=pl.ANY)
VMEM = pl.BlockSpec(memory_space=pltpu.VMEM)
SMEM = pl.BlockSpec(memory_space=pltpu.SMEM)
VMEM_BYTES = 56 * 1024 * 1024

HEADS = 16
HEAD = 48
WIDTH = 768
TOKENS = 768
BLOCK = 192
ROWS = 12
CHUNK = 6 * HEAD


def dot(left, right, contract=((1,), (0,))):
    return lax.dot_general(left, right, (contract, ((), ())), preferred_element_type=F32)


def norm_rows(values):
    center = values - jnp.mean(values, axis=-1, keepdims=True)
    inverse = lax.rsqrt(jnp.mean(center * center, axis=-1, keepdims=True) + EPSILON)
    return center * inverse, inverse


def norm_back(grad_in, normed, inverse):
    grad_mean = jnp.mean(grad_in, axis=-1, keepdims=True)
    cross_mean = jnp.mean(grad_in * normed, axis=-1, keepdims=True)
    return inverse * (grad_in - grad_mean - normed * cross_mean)


def iota(shape, dim):
    return lax.broadcasted_iota(jnp.int32, shape, dim)


class Place:
    def __init__(self):
        self.r = lax.axis_index("rows")
        self.b = lax.axis_index("grp")
        self.x = self.r // 16
        self.z = (self.r // 4) % 4
        self.y = self.r % 4
        self.me = self.y * 4 + self.b

    def group(self, k):
        peer = (self.me + k) % 16
        return peer, (self.r - self.y + peer // 4, peer % 4)

    def group_from(self, k):
        return (self.me + 16 - k) % 16

    def along(self, axis, k):
        if axis == "x":
            place = (self.x + k) % 4
            return place, (self.r + (place - self.x) * 16, self.b)
        if axis == "z":
            place = (self.z + k) % 4
            return place, (self.r + (place - self.z) * 4, self.b)
        place = (self.y + k) % 4
        return place, (self.r + (place - self.y), self.b)

    def along_from(self, axis, k):
        return ({"x": self.x, "z": self.z, "y": self.y}[axis] + 4 - k) % 4


def remote(source, target, send, recv, device):
    return pltpu.make_async_remote_copy(
        src_ref=source,
        dst_ref=target,
        send_sem=send,
        recv_sem=recv,
        device_id=device,
        device_id_type=MESH,
    )


def total_of(ref, rows=slice(None)):
    value = ref[0, rows, :].astype(F32)
    for n in range(1, 4):
        value = value + ref[n, rows, :].astype(F32)
    return value


def pair_bias(pair, chain_cols, chain_all, chain_gain, w_pair_t, at, bias_send):
    cols = chain_cols[...]
    mine = cols[:, :BLOCK]
    for b in range(1, 4):
        mine = jnp.where(at.b == b, cols[:, b * BLOCK : (b + 1) * BLOCK], mine)
    head = iota((HEADS, 1), 0)
    gain = jnp.zeros((HEADS, 1), F32)
    for h in range(HEADS):
        gain = jnp.where(head == h, chain_gain[h], gain)
    strips = []
    for i in range(ROWS):
        normed, _ = norm_rows(pair[i].astype(F32))
        projected = dot(w_pair_t[...], normed.astype(BF16), ((1,), (1,)))
        same = (mine == chain_all[at.r * ROWS + i]).astype(F32)
        strips.append((projected + gain * same).astype(BF16))
    strips = jnp.concatenate(strips, axis=0)
    shape = (HEADS * 16, HEADS * ROWS)
    to, source = iota(shape, 0), iota(shape, 1)
    order = ((to // 16 == source % 16) & (to % 16 == source // 16)).astype(BF16)
    spread = dot(order, strips).astype(BF16)
    for h in range(HEADS):
        rows = spread[h * 16 : (h + 1) * 16]
        bias_send[h, :, :128] = rows[:, :128]
        bias_send[h, :, 128:] = jnp.concatenate([rows[:, 128:], jnp.zeros((16, 64), BF16)], axis=1)


def make_acts(noised, cotangent, gamma, beta, gate, w_query, w_key, w_value, w_out, acts_send):
    noised_norm, _ = norm_rows(noised[...].astype(F32))
    x_b = (noised_norm * gamma + beta).astype(BF16)
    grad_update = (cotangent[...].astype(F32) * gate).astype(BF16)
    arrays = [
        dot(x_b, w_query[...]),
        dot(x_b, w_key[...]),
        dot(x_b, w_value[...]),
        dot(grad_update, w_out[...], ((1,), (1,))),
    ]
    pieces = [a[:128].T.astype(BF16) for a in arrays]
    for first, second in ((0, 2), (1, 3)):
        tail = jnp.concatenate([arrays[first][128:], arrays[second][128:]], axis=0)
        pieces.append(tail.T.astype(BF16))
    for h in range(HEADS):
        for n, piece in enumerate(pieces):
            acts_send[h, n * HEAD : (n + 1) * HEAD, :] = piece[h * HEAD : (h + 1) * HEAD]


def assemble_bias(held):
    strips = []
    for y in range(4):
        parts = [held[y * 4 + b] for b in range(4)]
        tails = [p[:, 128:BLOCK] for p in parts]
        strips.append(jnp.concatenate([p[:, :128] for p in parts] + tails, axis=1))
    strips = jnp.concatenate(strips, axis=0)
    to, source = iota((HEAD, 64), 0), iota((HEAD, 64), 1)
    pick = ((source // 16 == to // ROWS) & (source % 16 == to % ROWS)).astype(BF16)
    return dot(pick, strips).astype(BF16)


def spread_bias(total, to_group):
    to, source = iota((64, HEAD), 0), iota((64, HEAD), 1)
    pick = ((to // 16 == source // ROWS) & (to % 16 == source % ROWS)).astype(BF16)
    spread = dot(pick, total).astype(BF16)
    for y in range(4):
        rows = spread[y * 16 : (y + 1) * 16]
        for b in range(4):
            tail = rows[:, 512 + b * 64 : 512 + (b + 1) * 64]
            to_group[y * 4 + b, :, :128] = rows[:, b * 128 : (b + 1) * 128]
            to_group[y * 4 + b, :, 128:] = jnp.concatenate([tail, jnp.zeros_like(tail)], axis=1)


def half(n):
    return slice(n * 64, n * 64 + 64)


def wide(acts, first, n, tail, part):
    parts = [acts[first + b, n * HEAD : (n + 1) * HEAD, :] for b in range(4)]
    parts += [acts[first + b, tail * HEAD : (tail + 1) * HEAD, half(part)] for b in range(4)]
    return jnp.concatenate(parts, axis=1)


def block(acts, place, n, tail, part):
    return jnp.concatenate(
        [
            acts[place, n * HEAD : (n + 1) * HEAD, :],
            acts[place, tail * HEAD : (tail + 1) * HEAD, half(part)],
        ],
        axis=1,
    )


def attend(query_t, grad_t, key_t, value_t, bias):
    scale = 1.0 / math.sqrt(HEAD)
    query = query_t.astype(F32).T.astype(BF16)
    grad = grad_t.astype(F32).T.astype(BF16)
    scores = dot(query, key_t) * (scale * LOG2E) + bias
    weight = jnp.exp2(scores)
    prob = weight * (1.0 / jnp.sum(weight, axis=-1, keepdims=True))
    grad_prob = dot(grad, value_t)
    scaled = prob * grad_prob
    grad_score = scaled - prob * jnp.sum(scaled, axis=-1, keepdims=True)
    return prob.astype(BF16), grad_score.astype(BF16), grad_score


def back_piece(grads, n):
    rows = [grads[h, n * HEAD : (n + 1) * HEAD, :] for h in range(HEADS)]
    return jnp.concatenate(rows, axis=0).astype(F32).T.astype(BF16)


def pair_weight(w_pair_t):
    shape = (HEADS * 16, HEADS)
    pick = (iota(shape, 0) // 16 == iota(shape, 1)).astype(BF16)
    return dot(pick, w_pair_t[...]).astype(BF16)


def pair_back(grad_t, weight, pair, result, rows):
    row = iota(weight.shape, 0) % 16
    for i in rows:
        grad = dot(grad_t, jnp.where(row == i, weight, jnp.zeros_like(weight)))
        normed, inverse = norm_rows(pair[i].astype(F32))
        result[i] = norm_back(grad, normed, inverse).astype(BF16)


def block_kernel(
    single_in, pair_in, noised_in, cotangent_in,
    w_gamma_in, w_beta_in, w_outgate_in, w_query_in, w_key_in, w_value_in, w_out_in,
    chain_all, chain_cols, chain_gain, w_pair_t,
    updated, d_single, d_pair,
    single, pair, noised, cotangent, w_gamma, w_beta, w_outgate, w_query, w_key, w_value, w_out,
    bias_send, held, bias_all, acts_send, acts_all, gamma_v, gate_v,
    key_t, value_t, grad_key, grad_value, bias_f,
    to_x, from_x, to_z, from_z, to_group, from_group, grads_send, grads_all,
    part, sum_y, sum_z, sum_x, own,
    load, a_send, a_recv, b_send, b_recv, g_send, g_recv, h_send, h_recv, s_send, s_recv, r_send, r_recv,
):
    at = Place()
    barrier = pltpu.get_barrier_semaphore()
    peers = (
        [at.group(k)[1] for k in range(1, 16)]
        + [at.along("z", k)[1] for k in range(1, 4)]
        + [at.along("x", k)[1] for k in range(1, 4)]
    )
    for device in peers:
        pl.semaphore_signal(barrier, inc=1, device_id=device, device_id_type=MESH)
    loads = {}
    for n, (name, source, target) in enumerate(
        (
            ("pair", pair_in, pair),
            ("single", single_in, single),
            ("gamma", w_gamma_in, w_gamma),
            ("beta", w_beta_in, w_beta),
            ("gate", w_outgate_in, w_outgate),
            ("noised", noised_in, noised),
            ("query", w_query_in, w_query),
            ("key", w_key_in, w_key),
            ("value", w_value_in, w_value),
            ("cot", cotangent_in, cotangent),
            ("out", w_out_in, w_out),
        )
    ):
        loads[name] = pltpu.make_async_copy(source, target, load.at[n])
        loads[name].start()
    out = []

    def send(source, target, ssem, rsem, device):
        copy = remote(source, target, ssem, rsem, device)
        copy.start()
        out.append(copy)

    def arrive(buffer, ssem, rsem):
        remote(buffer, buffer, ssem, rsem, at.group(1)[1]).wait_recv()

    loads["pair"].wait()
    pair_bias(pair, chain_cols, chain_all, chain_gain, w_pair_t, at, bias_send)
    pl.semaphore_wait(barrier, len(peers))
    for k in range(1, 16):
        peer, device = at.group(k)
        send(bias_send.at[peer], held.at[at.me], b_send.at[k], b_recv.at[k], device)
    held[at.me] = bias_send[at.me]

    for name in ("single", "gamma", "beta", "gate", "noised", "query", "key", "value", "cot", "out"):
        loads[name].wait()
    single_norm, _ = norm_rows(single[...].astype(F32))
    single_b = single_norm.astype(BF16)
    gamma = jax.nn.sigmoid(dot(single_b, w_gamma[...]))
    beta = dot(single_b, w_beta[...])
    gate = jax.nn.sigmoid(dot(single_b, w_outgate[...]))
    gamma_v[...] = gamma
    gate_v[...] = gate
    make_acts(noised, cotangent, gamma, beta, gate, w_query, w_key, w_value, w_out, acts_send)

    for k in range(1, 16):
        arrive(held.at[at.group_from(k)], b_send.at[k], b_recv.at[k])
    bias_all[at.x, at.z] = assemble_bias(held)
    for k in range(1, 4):
        rows = bias_all.at[at.x, at.z]
        send(rows, rows, s_send.at[k], s_recv.at[k], at.along("z", k)[1])
    for k in range(1, 16):
        peer, device = at.group(k)
        send(acts_send.at[peer], acts_all.at[at.me], a_send.at[k], a_recv.at[k], device)
    acts_all[at.me] = acts_send[at.me]
    for k in range(1, 4):
        arrive(bias_all.at[at.x, at.along_from("z", k)], s_send.at[k], s_recv.at[k])
    for k in range(1, 4):
        rows = bias_all.at[at.x]
        send(rows, rows, s_send.at[4 + k], s_recv.at[4 + k], at.along("x", k)[1])
    for k in range(1, 16):
        arrive(acts_all.at[at.group_from(k)], a_send.at[k], a_recv.at[k])

    samples = [(at.y + 1 + s) % 4 for s in range(4)]
    for s in range(4):
        key_t[s] = wide(acts_all, samples[s] * 4, 1, 5, 0)
        value_t[s] = wide(acts_all, samples[s] * 4, 2, 4, 1)
        grad_key[s] = jnp.zeros((HEAD, TOKENS), F32)
        grad_value[s] = jnp.zeros((HEAD, TOKENS), F32)

    def step_body(step, carry):
        k = step + step // 2 - 2 * (step // 3)
        place, device = at.along("x", k)

        @pl.when(step > 0)
        def _():
            arrive(bias_all.at[place], s_send.at[8 - k], s_recv.at[8 - k])

        for z in range(4):
            bias_f[z * HEAD : (z + 1) * HEAD, :] = bias_all[place, z].astype(F32) * LOG2E
        found = []
        for s in range(4):
            slot = samples[s] * 4 + place
            query_t = block(acts_all, slot, 0, 4, 0)
            grad_t = block(acts_all, slot, 3, 5, 1)
            found.append((query_t, grad_t) + attend(query_t, grad_t, key_t[s], value_t[s], bias_f[...]))
        total = found[0][4]
        for s in range(1, 4):
            total = total + found[s][4]
        to_x[k] = total.astype(BF16)
        for s in range(4):
            query_t, grad_t, prob_b, score_b, _ = found[s]
            slot = samples[s] * 4 + place
            attended = dot(value_t[s], prob_b, ((1,), (1,))).astype(BF16)
            grad_query = dot(key_t[s], score_b, ((1,), (1,))) * (1.0 / math.sqrt(HEAD))
            grad_query = grad_query.astype(BF16)
            grad_value[s] = grad_value[s] + dot(grad_t, prob_b)
            grad_key[s] = grad_key[s] + dot(query_t, score_b)
            grads_send[slot, :HEAD, :] = attended[:, :128]
            grads_send[slot, HEAD : 2 * HEAD, :] = grad_query[:, :128]
            grads_send[slot, 4 * HEAD : 5 * HEAD, :64] = attended[:, 128:]
            grads_send[slot, 5 * HEAD :, :64] = grad_query[:, 128:]

        @pl.when(step > 0)
        def _():
            remote(to_x.at[k], from_x.at[at.x], s_send.at[8 + k], s_recv.at[8 + k], device).start()

        return carry

    lax.fori_loop(0, 4, step_body, 0)
    from_x[at.x] = to_x[0]
    for k in range(1, 4):
        out.append(
            remote(
                to_x.at[k], from_x.at[at.x], s_send.at[8 + k], s_recv.at[8 + k], at.along("x", k)[1]
            )
        )

    for s in range(4):
        key_b = (grad_key[s] * (1.0 / math.sqrt(HEAD))).astype(BF16)
        value_b = grad_value[s].astype(BF16)
        for b in range(4):
            slot = samples[s] * 4 + b
            lanes = slice(b * 128, (b + 1) * 128)
            tail = slice(512 + b * 64, 512 + (b + 1) * 64)
            grads_send[slot, 2 * HEAD : 3 * HEAD, :] = key_b[:, lanes]
            grads_send[slot, 3 * HEAD : 4 * HEAD, :] = value_b[:, lanes]
            grads_send[slot, 4 * HEAD : 5 * HEAD, 64:] = key_b[:, tail]
            grads_send[slot, 5 * HEAD :, 64:] = value_b[:, tail]
    for k in range(1, 16):
        peer, device = at.group(k)
        send(grads_send.at[peer], grads_all.at[at.me], g_send.at[k], g_recv.at[k], device)
    grads_all[at.me] = grads_send[at.me]

    for k in range(1, 4):
        arrive(from_x.at[at.along_from("x", k)], s_send.at[8 + k], s_recv.at[8 + k])
    for z in range(4):
        to_z[z] = total_of(from_x, slice(z * HEAD, (z + 1) * HEAD)).astype(BF16)
    for k in range(1, 4):
        place, device = at.along("z", k)
        send(to_z.at[place], from_z.at[at.z], s_send.at[12 + k], s_recv.at[12 + k], device)
    from_z[at.z] = to_z[at.z]
    for k in range(1, 4):
        arrive(from_z.at[at.along_from("z", k)], s_send.at[12 + k], s_recv.at[12 + k])
    spread_bias((total_of(from_z) * TOKENS).astype(BF16), to_group)
    for k in range(1, 16):
        peer, device = at.group(k)
        send(to_group.at[peer], from_group.at[at.me], h_send.at[k], h_recv.at[k], device)
    from_group[at.me] = to_group[at.me]

    for k in range(1, 16):
        arrive(grads_all.at[at.group_from(k)], g_send.at[k], g_recv.at[k])
    tails = [back_piece(grads_all, 4), back_piece(grads_all, 5)]
    attended = jnp.concatenate([back_piece(grads_all, 0), tails[0][:64]], axis=0)
    grad_q = jnp.concatenate([back_piece(grads_all, 1), tails[1][:64]], axis=0)
    grad_k = jnp.concatenate([back_piece(grads_all, 2), tails[0][64:]], axis=0)
    grad_v = jnp.concatenate([back_piece(grads_all, 3), tails[1][64:]], axis=0)
    gamma = gamma_v[...]
    gate = gate_v[...]
    block_update = dot(attended, w_out[...])
    noised_f = noised[...].astype(F32)
    updated[...] = (noised_f + gate * block_update).astype(BF16)
    noised_norm, _ = norm_rows(noised_f)
    back = ((1,), (1,))
    grad_input = (
        dot(grad_q, w_query[...], back) + dot(grad_k, w_key[...], back) + dot(grad_v, w_value[...], back)
    )
    pre_gamma = (grad_input * noised_norm * (gamma * (1.0 - gamma))).astype(BF16)
    pre_gate = (cotangent[...].astype(F32) * block_update * (gate * (1.0 - gate))).astype(BF16)
    sums = dot(pre_gamma, w_gamma[...], back)
    sums = sums + dot(grad_input.astype(BF16), w_beta[...], back)
    sums = sums + dot(pre_gate, w_outgate[...], back)
    sums = sums.astype(BF16)
    for y in range(4):
        part[y] = sums[y * HEAD : (y + 1) * HEAD]

    sum_y[at.y] = part[at.y]
    for k in range(1, 4):
        place, device = at.along("y", k)
        send(part.at[place], sum_y.at[at.y], r_send.at[k], r_recv.at[k], device)
    for k in range(1, 16):
        arrive(from_group.at[at.group_from(k)], h_send.at[k], h_recv.at[k])
    grad_t = jnp.concatenate([from_group[h] for h in range(HEADS)], axis=0)
    grad_t = grad_t.astype(F32).T.astype(BF16)[:BLOCK]
    weight = pair_weight(w_pair_t)
    pair_back(grad_t, weight, pair, d_pair, range(0, 4))
    for k in range(1, 4):
        arrive(sum_y.at[at.along_from("y", k)], r_send.at[k], r_recv.at[k])
    sum_z[at.z] = total_of(sum_y).astype(BF16)
    for k in range(1, 4):
        rows = sum_z.at[at.z]
        send(rows, rows, r_send.at[4 + k], r_recv.at[4 + k], at.along("z", k)[1])
    pair_back(grad_t, weight, pair, d_pair, range(4, 9))
    for k in range(1, 4):
        arrive(sum_z.at[at.along_from("z", k)], r_send.at[4 + k], r_recv.at[4 + k])
    sum_x[at.x] = total_of(sum_z).astype(BF16)
    for k in range(1, 4):
        rows = sum_x.at[at.x]
        send(rows, rows, r_send.at[8 + k], r_recv.at[8 + k], at.along("x", k)[1])
    pair_back(grad_t, weight, pair, d_pair, range(9, ROWS))
    normed, inverse = norm_rows(single[pl.ds(at.y * HEAD, HEAD), :].astype(F32))
    for k in range(1, 4):
        arrive(sum_x.at[at.along_from("x", k)], r_send.at[8 + k], r_recv.at[8 + k])
    final = norm_back(total_of(sum_x), normed, inverse)
    own[...] = final
    d_single[at.y] = final
    for k in range(1, 4):
        send(own, d_single.at[at.y], r_send.at[12 + k], r_recv.at[12 + k], at.along("y", k)[1])
    for k in range(1, 4):
        arrive(d_single.at[at.along_from("y", k)], r_send.at[12 + k], r_recv.at[12 + k])
    for copy in out:
        copy.wait_send()


def on_device(
    single,
    pair,
    chains,
    noised,
    w_gamma,
    w_beta,
    w_outgate,
    w_query,
    w_key,
    w_value,
    w_out,
    w_pair,
    chain_gain,
    cotangent,
):
    def space(*shape):
        return pltpu.VMEM(shape, BF16)

    def wide_space(*shape):
        return pltpu.VMEM(shape, F32)

    def dma(count):
        return pltpu.SemaphoreType.DMA((count,))

    half_width = WIDTH // 2
    updated, d_single, d_pair = pl.pallas_call(
        block_kernel,
        out_shape=[
            jax.ShapeDtypeStruct((BLOCK, WIDTH), BF16),
            jax.ShapeDtypeStruct((4, HEAD, half_width), F32),
            jax.ShapeDtypeStruct(pair.shape, BF16),
        ],
        in_specs=[ANY] * 11 + [SMEM, VMEM, SMEM, VMEM],
        out_specs=[VMEM] * 3,
        scratch_shapes=[
            space(BLOCK, half_width),
            space(ROWS, BLOCK, 128),
            space(BLOCK, WIDTH),
            space(BLOCK, WIDTH),
        ]
        + [space(half_width, WIDTH)] * 3
        + [space(WIDTH, WIDTH)] * 4
        + [
            space(16, 16, 256),
            space(16, 16, 256),
            space(4, 4, HEAD, TOKENS),
            space(16, CHUNK, 128),
            space(16, CHUNK, 128),
            wide_space(BLOCK, WIDTH),
            wide_space(BLOCK, WIDTH),
            space(4, HEAD, TOKENS),
            space(4, HEAD, TOKENS),
            wide_space(4, HEAD, TOKENS),
            wide_space(4, HEAD, TOKENS),
            wide_space(BLOCK, TOKENS),
            space(4, BLOCK, TOKENS),
            space(4, BLOCK, TOKENS),
            space(4, HEAD, TOKENS),
            space(4, HEAD, TOKENS),
            space(16, 16, 256),
            space(16, 16, 256),
            space(16, CHUNK, 128),
            space(16, CHUNK, 128),
        ]
        + [space(4, HEAD, half_width)] * 4
        + [wide_space(HEAD, half_width)]
        + [dma(11)]
        + [dma(16)] * 12,
        compiler_params=pltpu.CompilerParams(
            vmem_limit_bytes=VMEM_BYTES, collective_id=0, has_side_effects=True
        ),
        name="block",
    )(
        single,
        pair,
        noised.reshape(BLOCK, WIDTH),
        cotangent.reshape(BLOCK, WIDTH),
        w_gamma,
        w_beta,
        w_outgate,
        w_query,
        w_key,
        w_value,
        w_out,
        chains,
        chains.reshape(1, TOKENS),
        chain_gain,
        w_pair.T,
    )
    return (
        updated.reshape(1, BLOCK, WIDTH),
        d_single.reshape(BLOCK, half_width),
        d_pair,
    )


def solution(mesh):
    rows = P("rows", "grp", None)
    grp = P("grp", None)
    in_specs = (grp, rows, P(), rows) + (P(),) * 9 + (rows,)
    return jax.shard_map(
        on_device, mesh=mesh, in_specs=in_specs, out_specs=(rows, grp, rows), check_vma=False
    )
```

```python
import math

import jax
import jax.numpy as jnp
from jax import lax
from jax.experimental import pallas as pl
from jax.experimental.pallas import tpu as pltpu
from jax.sharding import PartitionSpec as P

EPSILON = 1e-05
LOG2E = math.log2(math.e)
F32 = jnp.float32
BF16 = jnp.bfloat16
MESH = pl.DeviceIdType.MESH
ANY = pl.BlockSpec(memory_space=pl.ANY)
VMEM = pl.BlockSpec(memory_space=pltpu.VMEM)
SMEM = pl.BlockSpec(memory_space=pltpu.SMEM)
VMEM_BYTES = 56 * 1024 * 1024

HEADS = 16
HEAD = 48
WIDTH = 768
TOKENS = 768
BLOCK = 192
ROWS = 12
CHUNK = 3 * HEAD


MIXED = (
    (1, 2), (3, 0), (2, 2), (1, 0), (3, 2), (2, 0), (0, 2), (0, 1),
    (1, 3), (3, 1), (2, 3), (1, 1), (3, 3), (2, 1), (0, 3),
)


def dot(left, right, contract=((1,), (0,))):
    return lax.dot_general(left, right, (contract, ((), ())), preferred_element_type=F32)


def norm_rows(values):
    center = values - jnp.mean(values, axis=-1, keepdims=True)
    inverse = lax.rsqrt(jnp.mean(center * center, axis=-1, keepdims=True) + EPSILON)
    return center * inverse, inverse


def norm_back(grad_in, normed, inverse):
    grad_mean = jnp.mean(grad_in, axis=-1, keepdims=True)
    cross_mean = jnp.mean(grad_in * normed, axis=-1, keepdims=True)
    return inverse * (grad_in - grad_mean - normed * cross_mean)


def iota(shape, dim):
    return lax.broadcasted_iota(jnp.int32, shape, dim)


class Place:
    def __init__(self):
        self.r = lax.axis_index("rows")
        self.b = lax.axis_index("grp")
        self.x = self.r // 16
        self.z = (self.r // 4) % 4
        self.y = self.r % 4
        self.me = self.y * 4 + self.b
        self.flip = 2 * (self.z % 2)
        self.head = self.y * 4 + (self.b + self.flip) % 4
        toward = 2 * (self.b // 2) - 1
        self.near = (self.z + 4 + toward) % 4
        self.far = (self.z + 4 - toward) % 4
        self.opposite = (self.z + 2) % 4

    def mate(self, dy, c):
        y = (self.y + dy) % 4
        b = (self.b + 2 * (c // 2)) % 4
        if c % 2:
            b = b + 1 - 2 * (b % 2)
        head = y * 4 + (b + self.flip) % 4
        return y * 4 + b, head, (self.r - self.y + y, b)

    def link(self, b):
        return 2 * ((self.b // 2 + b // 2) % 2) + (self.b + b) % 2

    def same_head(self, z):
        return (self.r + (z - self.z) * 4, (self.b + 2) % 4)

    def along(self, axis, k):
        if axis == "x":
            place = (self.x + k) % 4
            return place, (self.r + (place - self.x) * 16, self.b)
        if axis == "z":
            place = (self.z + k) % 4
            return place, (self.r + (place - self.z) * 4, self.b)
        place = (self.y + k) % 4
        return place, (self.r + (place - self.y), self.b)

    def along_from(self, axis, k):
        return ({"x": self.x, "z": self.z, "y": self.y}[axis] + 4 - k) % 4


def remote(source, target, send, recv, device):
    return pltpu.make_async_remote_copy(
        src_ref=source,
        dst_ref=target,
        send_sem=send,
        recv_sem=recv,
        device_id=device,
        device_id_type=MESH,
    )


def total_of(ref, rows=slice(None)):
    value = ref[0, rows, :].astype(F32)
    for n in range(1, 4):
        value = value + ref[n, rows, :].astype(F32)
    return value


def pair_bias(pair, chain_cols, chain_all, chain_gain, w_pair_t, at, bias_send):
    cols = chain_cols[...]
    mine = cols[:, :BLOCK]
    for b in range(1, 4):
        mine = jnp.where(at.b == b, cols[:, b * BLOCK : (b + 1) * BLOCK], mine)
    head = iota((HEADS, 1), 0)
    gain = jnp.zeros((HEADS, 1), F32)
    for h in range(HEADS):
        gain = jnp.where(head == h, chain_gain[h], gain)
    strips = []
    for i in range(ROWS):
        normed, _ = norm_rows(pair[i].astype(F32))
        projected = dot(w_pair_t[...], normed.astype(BF16), ((1,), (1,)))
        same = (mine == chain_all[at.r * ROWS + i]).astype(F32)
        strips.append((projected + gain * same).astype(BF16))
    strips = jnp.concatenate(strips, axis=0)
    shape = (HEADS * 16, HEADS * ROWS)
    to, source = iota(shape, 0), iota(shape, 1)
    order = ((to // 16 == source % 16) & (to % 16 == source // 16)).astype(BF16)
    spread = dot(order, strips).astype(BF16)
    for h in range(HEADS):
        rows = spread[h * 16 : (h + 1) * 16]
        bias_send[h, :, :128] = rows[:, :128]
        bias_send[h, :, 128:] = jnp.concatenate([rows[:, 128:], jnp.zeros((16, 64), BF16)], axis=1)


def make_acts(noised, cotangent, gamma, beta, gate, w_query, w_key, w_value, w_out, acts_send):
    noised_norm, _ = norm_rows(noised[...].astype(F32))
    x_b = (noised_norm * gamma + beta).astype(BF16)
    grad_update = (cotangent[...].astype(F32) * gate).astype(BF16)
    arrays = (
        (dot(x_b, w_key[...]), dot(x_b, w_value[...])),
        (dot(x_b, w_query[...]), dot(grad_update, w_out[...], ((1,), (1,)))),
    )
    for part, (first, second) in enumerate(arrays):
        tail = jnp.concatenate([first[128:], second[128:]], axis=0)
        for n, piece in enumerate((first[:128], second[:128], tail)):
            piece = piece.T.astype(BF16)
            for h in range(HEADS):
                acts_send[h, part, n * HEAD : (n + 1) * HEAD, :] = piece[h * HEAD : (h + 1) * HEAD]


def assemble_bias(held):
    strips = []
    for y in range(4):
        parts = [held[y * 4 + b] for b in range(4)]
        tails = [p[:, 128:BLOCK] for p in parts]
        strips.append(jnp.concatenate([p[:, :128] for p in parts] + tails, axis=1))
    strips = jnp.concatenate(strips, axis=0)
    to, source = iota((HEAD, 64), 0), iota((HEAD, 64), 1)
    pick = ((source // 16 == to // ROWS) & (source % 16 == to % ROWS)).astype(BF16)
    return dot(pick, strips).astype(BF16)


def spread_bias(total, to_group):
    to, source = iota((64, HEAD), 0), iota((64, HEAD), 1)
    pick = ((to // 16 == source // ROWS) & (to % 16 == source % ROWS)).astype(BF16)
    spread = dot(pick, total).astype(BF16)
    for y in range(4):
        rows = spread[y * 16 : (y + 1) * 16]
        for b in range(4):
            tail = rows[:, 512 + b * 64 : 512 + (b + 1) * 64]
            to_group[y * 4 + b, :, :128] = rows[:, b * 128 : (b + 1) * 128]
            to_group[y * 4 + b, :, 128:] = jnp.concatenate([tail, jnp.zeros_like(tail)], axis=1)


def half(n):
    return slice(n * 64, n * 64 + 64)


def wide(acts, first, n):
    parts = [acts[first + b, 0, n * HEAD : (n + 1) * HEAD, :] for b in range(4)]
    parts += [acts[first + b, 0, 2 * HEAD :, half(n)] for b in range(4)]
    return jnp.concatenate(parts, axis=1)


def block(acts, place, n):
    return jnp.concatenate(
        [acts[place, 1, n * HEAD : (n + 1) * HEAD, :], acts[place, 1, 2 * HEAD :, half(n)]], axis=1
    )


def attend(query_t, grad_t, key_t, value_t, bias):
    scale = 1.0 / math.sqrt(HEAD)
    query = query_t.astype(F32).T.astype(BF16)
    grad = grad_t.astype(F32).T.astype(BF16)
    scores = dot(query, key_t) * (scale * LOG2E) + bias
    weight = jnp.exp2(scores)
    prob = weight * (1.0 / jnp.sum(weight, axis=-1, keepdims=True))
    grad_prob = dot(grad, value_t)
    scaled = prob * grad_prob
    grad_score = scaled - prob * jnp.sum(scaled, axis=-1, keepdims=True)
    return prob.astype(BF16), grad_score.astype(BF16), grad_score


def back_pieces(grads, part):
    def piece(n):
        rows = [grads[h, part, n * HEAD : (n + 1) * HEAD, :] for h in range(HEADS)]
        return jnp.concatenate(rows, axis=0).astype(F32).T.astype(BF16)

    tail = piece(2)
    return [jnp.concatenate([piece(n), tail[n * 64 : n * 64 + 64]], axis=0) for n in (0, 1)]


def pair_weight(w_pair_t):
    shape = (HEADS * 16, HEADS)
    pick = (iota(shape, 0) // 16 == iota(shape, 1)).astype(BF16)
    return dot(pick, w_pair_t[...]).astype(BF16)


def pair_back(grad_t, weight, pair, result, rows):
    row = iota(weight.shape, 0) % 16
    for i in rows:
        grad = dot(grad_t, jnp.where(row == i, weight, jnp.zeros_like(weight)))
        normed, inverse = norm_rows(pair[i].astype(F32))
        result[i] = norm_back(grad, normed, inverse).astype(BF16)


def block_kernel(
    single_in, pair_in, noised_in, cotangent_in,
    w_gamma_in, w_beta_in, w_outgate_in, w_query_in, w_key_in, w_value_in, w_out_in,
    chain_in, cols_in, gain_in, w_pair_in,
    updated_out, d_single, d_pair_out,
    single, pair, noised, cotangent, w_gamma, w_beta, w_outgate, w_query, w_key, w_value, w_out,
    bias_send, held, bias_all, acts_send, acts_all, gamma_v, gate_v, bias_f,
    key_t, value_t, grad_key, grad_value,
    to_x, from_x, to_z, from_z, to_group, from_group, grads_send, grads_all,
    part, sum_y, sum_z, sum_x, updated, d_pair, sums_v, inner_v, chain_all, chain_cols, chain_gain, w_pair_t,
    load, a_send, a_recv, q_send, q_recv, b_send, b_recv, g_send, g_recv, o_send, o_recv, h_send, h_recv,
    x_send, x_recv, u_send, u_recv, z_send, z_recv, r_send, r_recv,
):
    at = Place()
    barrier = pltpu.get_barrier_semaphore()
    mates = [(dy, c) for dy in (1, 2, 3, 0) for c in (2, 3, 0, 1) if (dy, c) != (0, 0)]
    peers = (
        [at.along("z", k)[1] for k in (2, 1, 3)]
        + [at.same_head(at.far), at.same_head(at.near)]
        + [at.along("x", k)[1] for k in (2, 1, 3)]
        + [at.mate(dy, c)[2] for dy, c in mates]
    )
    for device in peers:
        pl.semaphore_signal(barrier, inc=1, device_id=device, device_id_type=MESH)
    loads = {}
    for n, (name, source, target) in enumerate(
        (
            ("chain", chain_in, chain_all),
            ("gain", gain_in, chain_gain),
            ("cols", cols_in, chain_cols),
            ("map", w_pair_in, w_pair_t),
            ("pair", pair_in, pair),
            ("single", single_in, single),
            ("gamma", w_gamma_in, w_gamma),
            ("beta", w_beta_in, w_beta),
            ("gate", w_outgate_in, w_outgate),
            ("noised", noised_in, noised),
            ("query", w_query_in, w_query),
            ("key", w_key_in, w_key),
            ("value", w_value_in, w_value),
            ("cot", cotangent_in, cotangent),
            ("out", w_out_in, w_out),
        )
    ):
        loads[name] = pltpu.make_async_copy(source, target, load.at[n])
        loads[name].start()
    out = []

    def send(source, target, ssem, rsem, device):
        copy = remote(source, target, ssem, rsem, device)
        copy.start()
        out.append(copy)

    def arrive(buffer, ssem, rsem):
        remote(buffer, buffer, ssem, rsem, at.along("x", 1)[1]).wait_recv()

    def send_acts(part, dy, c):
        _, head, device = at.mate(dy, c)
        n = dy * 4 + c
        ssem, rsem = ((a_send, a_recv), (q_send, q_recv))[part]
        send(acts_send.at[head, part], acts_all.at[at.me, part], ssem.at[n], rsem.at[n], device)

    def send_all_acts(part):
        for dy, c in MIXED:
            send_acts(part, dy, c)

    for name in ("chain", "gain", "cols", "map", "pair"):
        loads[name].wait()
    pair_bias(pair, chain_cols, chain_all, chain_gain, w_pair_t, at, bias_send)
    pl.semaphore_wait(barrier, len(peers))
    for dy, c in mates:
        _, head, device = at.mate(dy, c)
        n = dy * 4 + c
        send(bias_send.at[head], held.at[at.me], b_send.at[n], b_recv.at[n], device)
    held[at.me] = bias_send[at.head]
    for name in ("single", "gamma", "beta", "gate", "noised", "query", "key", "value", "cot", "out"):
        loads[name].wait()
    single_norm, _ = norm_rows(single[...].astype(F32))
    single_b = single_norm.astype(BF16)
    gamma = jax.nn.sigmoid(dot(single_b, w_gamma[...]))
    beta = dot(single_b, w_beta[...])
    gate = jax.nn.sigmoid(dot(single_b, w_outgate[...]))
    gamma_v[...] = gamma
    gate_v[...] = gate
    make_acts(noised, cotangent, gamma, beta, gate, w_query, w_key, w_value, w_out, acts_send)
    send_all_acts(0)
    acts_all[at.me] = acts_send[at.head]
    for dy, c in mates:
        n = dy * 4 + c
        arrive(held.at[at.mate(4 - dy, c)[0]], b_send.at[n], b_recv.at[n])
    bias_all[at.x, at.z] = assemble_bias(held)
    order = (at.z, at.near, at.far, at.opposite)
    rows = bias_all.at[at.x, at.z]
    send(rows, rows, z_send.at[2], z_recv.at[2], at.same_head(at.far))
    send(rows, rows, z_send.at[1], z_recv.at[1], at.same_head(at.near))
    for kz in range(4):
        rows = bias_all.at[at.x, order[kz]]
        if kz:
            arrive(rows, z_send.at[kz], z_recv.at[kz])
        if kz == 2:
            send(rows, rows, z_send.at[3], z_recv.at[3], at.same_head(at.near))
        for k in (2, 1, 3):
            n = k * 4 + kz
            send(rows, rows, x_send.at[n], x_recv.at[n], at.along("x", k)[1])
        if kz == 0:
            send_all_acts(1)
    samples = [(at.y + 4 - dy) % 4 for dy in (1, 2, 3, 0)]
    for s, dy in enumerate((1, 2, 3, 0)):
        for c in range(4):
            if dy or c:
                n = dy * 4 + c
                arrive(acts_all.at[at.mate(4 - dy, c)[0], 0], a_send.at[n], a_recv.at[n])
        key_t[s] = wide(acts_all, samples[s] * 4, 0)
        value_t[s] = wide(acts_all, samples[s] * 4, 1)
        grad_key[s] = jnp.zeros((HEAD, TOKENS), F32)
        grad_value[s] = jnp.zeros((HEAD, TOKENS), F32)

    scale = 1.0 / math.sqrt(HEAD)

    def step_body(step, carry):
        k = step + step // 2 - 2 * (step // 3)
        place, device = at.along("x", k)
        c = at.link(place)

        @pl.when(step > 0)
        def _():
            for kz in range(4):
                n = (4 - k) * 4 + kz
                arrive(bias_all.at[place, order[kz]], x_send.at[n], x_recv.at[n])

        @pl.when(c > 0)
        def _():
            arrive(acts_all.at[at.y * 4 + place, 1], q_send.at[c], q_recv.at[c])

        for s, dy in enumerate((1, 2, 3)):
            n = dy * 4 + c
            arrive(acts_all.at[samples[s] * 4 + place, 1], q_send.at[n], q_recv.at[n])
        for z in range(4):
            bias_f[z * HEAD : (z + 1) * HEAD, :] = bias_all[place, z].astype(F32) * LOG2E

        def weigh(s):
            slot = samples[s] * 4 + place
            query_t = block(acts_all, slot, 0)
            grad_t = block(acts_all, slot, 1)
            return (query_t, grad_t) + attend(query_t, grad_t, key_t[s], value_t[s], bias_f[...])

        ahead = weigh(0)
        total = ahead[4]
        for s, dy in enumerate((1, 2, 3, 0)):
            query_t, grad_t, prob_b, score_b, _ = ahead
            if s < 3:
                ahead = weigh(s + 1)
                total = total + ahead[4]
            slot = samples[s] * 4 + place
            attended = dot(value_t[s], prob_b, ((1,), (1,))).astype(BF16)
            grad_query = (dot(key_t[s], score_b, ((1,), (1,))) * scale).astype(BF16)
            grad_value[s] = grad_value[s] + dot(grad_t, prob_b)
            grad_key[s] = grad_key[s] + dot(query_t, score_b)
            grads_send[slot, 1, :HEAD, :] = attended[:, :128]
            grads_send[slot, 1, HEAD : 2 * HEAD, :] = grad_query[:, :128]
            grads_send[slot, 1, 2 * HEAD :, :64] = attended[:, 128:]
            grads_send[slot, 1, 2 * HEAD :, 64:] = grad_query[:, 128:]
        for z in range(4):
            to_x[k, z] = total[z * HEAD : (z + 1) * HEAD].astype(BF16)

        @pl.when(step > 0)
        def _():
            for kz in (3, 2, 1, 0):
                z = order[kz]
                n = k * 4 + kz
                remote(to_x.at[k, z], from_x.at[at.x, z], u_send.at[n], u_recv.at[n], device).start()

        for s, dy in enumerate((1, 2, 3, 0)):
            slot = samples[s] * 4 + place
            n = (4 - dy) % 4 * 4 + c
            copy = remote(
                grads_send.at[slot, 1],
                grads_all.at[at.head, 1],
                o_send.at[n],
                o_recv.at[n],
                (at.r - at.y + samples[s], place),
            )
            if dy:
                copy.start()
            else:
                pl.when(c > 0)(copy.start)
        return carry

    lax.fori_loop(0, 4, step_body, 0)
    for s, dy in enumerate((1, 2, 3, 0)):
        key_b = (grad_key[s] * scale).astype(BF16)
        value_b = grad_value[s].astype(BF16)
        for b in range(4):
            slot = samples[s] * 4 + b
            lanes = slice(b * 128, (b + 1) * 128)
            tail = slice(512 + b * 64, 512 + (b + 1) * 64)
            grads_send[slot, 0, :HEAD, :] = key_b[:, lanes]
            grads_send[slot, 0, HEAD : 2 * HEAD, :] = value_b[:, lanes]
            grads_send[slot, 0, 2 * HEAD :, :64] = key_b[:, tail]
            grads_send[slot, 0, 2 * HEAD :, 64:] = value_b[:, tail]
        for c in (2, 0, 3, 1):
            if dy or c:
                slot, _, device = at.mate(4 - dy, c)
                n = (4 - dy) % 4 * 4 + c
                send(
                    grads_send.at[slot, 0], grads_all.at[at.head, 0], g_send.at[n], g_recv.at[n], device
                )
    for dy, c in mates:
        slot, _, device = at.mate(dy, c)
        n = dy * 4 + c
        out.append(
            remote(grads_send.at[slot, 1], grads_all.at[at.head, 1], o_send.at[n], o_recv.at[n], device)
        )
    for k in range(1, 4):
        for kz in range(4):
            z = order[kz]
            n = k * 4 + kz
            device = at.along("x", k)[1]
            out.append(remote(to_x.at[k, z], from_x.at[at.x, z], u_send.at[n], u_recv.at[n], device))
    grads_all[at.head] = grads_send[at.me]
    from_x[at.x] = to_x[0]

    for dy, c in mates:
        n = dy * 4 + c
        arrive(grads_all.at[at.mate(4 - dy, c)[1], 1], o_send.at[n], o_recv.at[n])
    attended, grad_q = back_pieces(grads_all, 1)
    gamma = gamma_v[...]
    gate = gate_v[...]
    block_update = dot(attended, w_out[...])
    noised_f = noised[...].astype(F32)
    updated[...] = (noised_f + gate * block_update).astype(BF16)
    noised_norm, _ = norm_rows(noised_f)
    back = ((1,), (1,))
    pre_gate = (cotangent[...].astype(F32) * block_update * (gate * (1.0 - gate))).astype(BF16)
    sums_v[...] = dot(pre_gate, w_outgate[...], back)
    inner_v[...] = dot(grad_q, w_query[...], back)
    gamma_v[...] = noised_norm * (gamma * (1.0 - gamma))
    save = pltpu.make_async_copy(updated, updated_out, load.at[0])
    save.start()

    def rows_for(kz):
        z = order[kz]
        for k in range(1, 4):
            n = k * 4 + kz
            arrive(from_x.at[at.along_from("x", k), z], u_send.at[n], u_recv.at[n])
        rows = from_x[0, z].astype(F32)
        for x in range(1, 4):
            rows = rows + from_x[x, z].astype(F32)
        return rows

    to_z[3] = rows_for(3).astype(BF16)
    send(to_z.at[3], from_z.at[3], z_send.at[7], z_recv.at[7], at.same_head(at.near))
    to_z[1] = rows_for(1).astype(BF16)
    send(to_z.at[1], from_z.at[1], z_send.at[5], z_recv.at[5], at.same_head(at.near))
    for dy, c in mates:
        n = dy * 4 + c
        arrive(grads_all.at[at.mate(4 - dy, c)[1], 0], g_send.at[n], g_recv.at[n])
    grad_k, grad_v = back_pieces(grads_all, 0)
    grad_input = inner_v[...] + dot(grad_k, w_key[...], back) + dot(grad_v, w_value[...], back)
    pre_gamma = (grad_input * gamma_v[...]).astype(BF16)
    sums = sums_v[...] + dot(pre_gamma, w_gamma[...], back)
    sums = sums + dot(grad_input.astype(BF16), w_beta[...], back)
    sums = sums.astype(BF16)
    for y in range(4):
        part[y] = sums[y * HEAD : (y + 1) * HEAD]
    for k in (2, 1, 3):
        place, device = at.along("y", k)
        send(part.at[place], sum_y.at[at.y], r_send.at[k], r_recv.at[k], device)
    sum_y[at.y] = part[at.y]

    to_far = rows_for(2)
    arrive(from_z.at[3], z_send.at[7], z_recv.at[7])
    to_z[2] = (to_far + from_z[3].astype(F32)).astype(BF16)
    send(to_z.at[2], from_z.at[2], z_send.at[6], z_recv.at[6], at.same_head(at.far))
    for k in range(1, 4):
        arrive(sum_y.at[at.along_from("y", k)], r_send.at[k], r_recv.at[k])
    sum_z[at.z] = total_of(sum_y).astype(BF16)
    for k in (2, 1, 3):
        rows = sum_z.at[at.z]
        send(rows, rows, r_send.at[4 + k], r_recv.at[4 + k], at.along("z", k)[1])
    own_rows = rows_for(0)
    weight = pair_weight(w_pair_t)
    normed, inverse = norm_rows(single[pl.ds(at.y * HEAD, HEAD), :].astype(F32))
    for kz in (1, 2):
        arrive(from_z.at[kz], z_send.at[4 + kz], z_recv.at[4 + kz])
    own_rows = own_rows + from_z[1].astype(F32) + from_z[2].astype(F32)
    spread_bias((own_rows * TOKENS).astype(BF16), to_group)
    for dy, c in mates:
        slot, _, device = at.mate(dy, c)
        n = dy * 4 + c
        send(to_group.at[slot], from_group.at[at.head], h_send.at[n], h_recv.at[n], device)
    from_group[at.head] = to_group[at.me]
    for k in range(1, 4):
        arrive(sum_z.at[at.along_from("z", k)], r_send.at[4 + k], r_recv.at[4 + k])
    sum_x[at.x] = total_of(sum_z).astype(BF16)
    for k in (2, 1, 3):
        rows = sum_x.at[at.x]
        send(rows, rows, r_send.at[8 + k], r_recv.at[8 + k], at.along("x", k)[1])
    for dy, c in mates:
        n = dy * 4 + c
        arrive(from_group.at[at.mate(4 - dy, c)[1]], h_send.at[n], h_recv.at[n])
    grad_t = jnp.concatenate([from_group[h] for h in range(HEADS)], axis=0)
    grad_t = grad_t.astype(F32).T.astype(BF16)[:BLOCK]
    pair_back(grad_t, weight, pair, d_pair, range(0, 6))
    for k in range(1, 4):
        arrive(sum_x.at[at.along_from("x", k)], r_send.at[8 + k], r_recv.at[8 + k])
    d_single[at.y] = norm_back(total_of(sum_x), normed, inverse).astype(BF16)
    for k in (2, 1, 3):
        rows = d_single.at[at.y]
        send(rows, rows, r_send.at[12 + k], r_recv.at[12 + k], at.along("y", k)[1])
    pair_back(grad_t, weight, pair, d_pair, range(6, ROWS))
    keep = pltpu.make_async_copy(d_pair, d_pair_out, load.at[1])
    keep.start()
    save.wait()
    keep.wait()
    for k in range(1, 4):
        arrive(d_single.at[at.along_from("y", k)], r_send.at[12 + k], r_recv.at[12 + k])
    for copy in out:
        copy.wait_send()


def finish_kernel(updated_in, d_single_in, d_pair_in, updated, d_single, d_pair):
    updated[...] = updated_in[...]
    d_single[...] = d_single_in[...].astype(F32)
    d_pair[...] = d_pair_in[...]


def on_device(
    single,
    pair,
    chains,
    noised,
    w_gamma,
    w_beta,
    w_outgate,
    w_query,
    w_key,
    w_value,
    w_out,
    w_pair,
    chain_gain,
    cotangent,
):
    def space(*shape):
        return pltpu.VMEM(shape, BF16)

    def wide_space(*shape):
        return pltpu.VMEM(shape, F32)

    def dma(count):
        return pltpu.SemaphoreType.DMA((count,))

    half_width = WIDTH // 2
    results = pl.pallas_call(
        block_kernel,
        out_shape=[
            jax.ShapeDtypeStruct((BLOCK, WIDTH), BF16),
            jax.ShapeDtypeStruct((4, HEAD, half_width), BF16),
            jax.ShapeDtypeStruct(pair.shape, BF16),
        ],
        in_specs=[ANY] * 15,
        out_specs=[ANY, VMEM, ANY],
        scratch_shapes=[
            space(BLOCK, half_width),
            space(ROWS, BLOCK, 128),
            space(BLOCK, WIDTH),
            space(BLOCK, WIDTH),
        ]
        + [space(half_width, WIDTH)] * 3
        + [space(WIDTH, WIDTH)] * 4
        + [
            space(16, 16, 256),
            space(16, 16, 256),
            space(4, 4, HEAD, TOKENS),
            space(16, 2, CHUNK, 128),
            space(16, 2, CHUNK, 128),
            wide_space(BLOCK, WIDTH),
            wide_space(BLOCK, WIDTH),
            wide_space(BLOCK, TOKENS),
            space(4, HEAD, TOKENS),
            space(4, HEAD, TOKENS),
            wide_space(4, HEAD, TOKENS),
            wide_space(4, HEAD, TOKENS),
            space(4, 4, HEAD, TOKENS),
            space(4, 4, HEAD, TOKENS),
            space(4, HEAD, TOKENS),
            space(4, HEAD, TOKENS),
            space(16, 16, 256),
            space(16, 16, 256),
            space(16, 2, CHUNK, 128),
            space(16, 2, CHUNK, 128),
        ]
        + [space(4, HEAD, half_width)] * 4
        + [space(BLOCK, WIDTH), space(ROWS, BLOCK, 128)]
        + [wide_space(BLOCK, half_width), wide_space(BLOCK, WIDTH)]
        + [
            pltpu.SMEM((TOKENS,), jnp.int32),
            pltpu.VMEM((1, TOKENS), jnp.int32),
            pltpu.SMEM((HEADS,), F32),
            space(HEADS, 128),
        ]
        + [dma(15)]
        + [dma(16)] * 20,
        compiler_params=pltpu.CompilerParams(
            vmem_limit_bytes=VMEM_BYTES, collective_id=0, has_side_effects=True
        ),
        name="block",
    )(
        single,
        pair,
        noised.reshape(BLOCK, WIDTH),
        cotangent.reshape(BLOCK, WIDTH),
        w_gamma,
        w_beta,
        w_outgate,
        w_query,
        w_key,
        w_value,
        w_out,
        chains,
        chains.reshape(1, TOKENS),
        chain_gain,
        w_pair.T,
    )
    updated, d_single, d_pair = pl.pallas_call(
        finish_kernel,
        out_shape=[
            jax.ShapeDtypeStruct((BLOCK, WIDTH), BF16),
            jax.ShapeDtypeStruct((BLOCK, half_width), F32),
            jax.ShapeDtypeStruct(pair.shape, BF16),
        ],
        in_specs=[VMEM] * 3,
        out_specs=[VMEM] * 3,
        name="finish",
    )(results[0], results[1].reshape(BLOCK, half_width), results[2])
    return updated.reshape(1, BLOCK, WIDTH), d_single, d_pair


def solution(mesh):
    rows = P("rows", "grp", None)
    grp = P("grp", None)
    in_specs = (grp, rows, P(), rows) + (P(),) * 9 + (rows,)
    return jax.shard_map(
        on_device, mesh=mesh, in_specs=in_specs, out_specs=(rows, grp, rows), check_vma=False
    )
```

```python
import math

import jax
import jax.numpy as jnp
from jax import lax
from jax.experimental import pallas as pl
from jax.experimental.pallas import tpu as pltpu
from jax.sharding import PartitionSpec as P

EPSILON = 1e-05
LOG2E = math.log2(math.e)
F32 = jnp.float32
BF16 = jnp.bfloat16
MESH = pl.DeviceIdType.MESH
ANY = pl.BlockSpec(memory_space=pl.ANY)
VMEM = pl.BlockSpec(memory_space=pltpu.VMEM)
SMEM = pl.BlockSpec(memory_space=pltpu.SMEM)
VMEM_BYTES = 56 * 1024 * 1024

HEADS = 16
HEAD = 48
WIDTH = 768
TOKENS = 768
BLOCK = 192
ROWS = 12
CHUNK = 3 * HEAD


MIXED = (
    (1, 2), (3, 0), (2, 2), (1, 0), (3, 2), (2, 0), (0, 2), (0, 1),
    (1, 3), (3, 1), (2, 3), (1, 1), (3, 3), (2, 1), (0, 3),
)


def dot(left, right, contract=((1,), (0,))):
    return lax.dot_general(left, right, (contract, ((), ())), preferred_element_type=F32)


def norm_rows(values):
    center = values - jnp.mean(values, axis=-1, keepdims=True)
    inverse = lax.rsqrt(jnp.mean(center * center, axis=-1, keepdims=True) + EPSILON)
    return center * inverse, inverse


def norm_back(grad_in, normed, inverse):
    grad_mean = jnp.mean(grad_in, axis=-1, keepdims=True)
    cross_mean = jnp.mean(grad_in * normed, axis=-1, keepdims=True)
    return inverse * (grad_in - grad_mean - normed * cross_mean)


def iota(shape, dim):
    return lax.broadcasted_iota(jnp.int32, shape, dim)


class Place:
    def __init__(self):
        self.r = lax.axis_index("rows")
        self.b = lax.axis_index("grp")
        self.x = self.r // 16
        self.z = (self.r // 4) % 4
        self.y = self.r % 4
        self.spot = self.x * 4 + self.y
        self.me = self.y * 4 + self.b
        self.flip = 2 * (self.z % 2)
        self.head = self.y * 4 + (self.b + self.flip) % 4
        toward = 2 * (self.b // 2) - 1
        self.near = (self.z + 4 + toward) % 4
        self.far = (self.z + 4 - toward) % 4
        self.opposite = (self.z + 2) % 4

    def mate(self, dy, c):
        y = (self.y + dy) % 4
        b = (self.b + 2 * (c // 2)) % 4
        if c % 2:
            b = b + 1 - 2 * (b % 2)
        head = y * 4 + (b + self.flip) % 4
        return y * 4 + b, head, (self.r - self.y + y, b)

    def link(self, b):
        return 2 * ((self.b // 2 + b // 2) % 2) + (self.b + b) % 2

    def same_head(self, z):
        return (self.r + (z - self.z) * 4, (self.b + 2) % 4)

    def plane(self, dx, dy):
        x, y = (self.x + dx) % 4, (self.y + dy) % 4
        return x * 4 + y, (self.r + (x - self.x) * 16 + (y - self.y), self.b)

    def along(self, axis, k):
        if axis == "x":
            place = (self.x + k) % 4
            return place, (self.r + (place - self.x) * 16, self.b)
        if axis == "z":
            place = (self.z + k) % 4
            return place, (self.r + (place - self.z) * 4, self.b)
        place = (self.y + k) % 4
        return place, (self.r + (place - self.y), self.b)

    def along_from(self, axis, k):
        return ({"x": self.x, "z": self.z, "y": self.y}[axis] + 4 - k) % 4


def remote(source, target, send, recv, device):
    return pltpu.make_async_remote_copy(
        src_ref=source,
        dst_ref=target,
        send_sem=send,
        recv_sem=recv,
        device_id=device,
        device_id_type=MESH,
    )


def total_of(ref, rows=slice(None)):
    value = ref[0, rows, :].astype(F32)
    for n in range(1, 4):
        value = value + ref[n, rows, :].astype(F32)
    return value


def pair_bias(pair, chain_cols, chain_all, chain_gain, w_pair_t, at, bias_send):
    cols = chain_cols[...]
    mine = cols[:, :BLOCK]
    for b in range(1, 4):
        mine = jnp.where(at.b == b, cols[:, b * BLOCK : (b + 1) * BLOCK], mine)
    head = iota((HEADS, 1), 0)
    gain = jnp.zeros((HEADS, 1), F32)
    for h in range(HEADS):
        gain = jnp.where(head == h, chain_gain[h], gain)
    strips = []
    for i in range(ROWS):
        normed, _ = norm_rows(pair[i].astype(F32))
        projected = dot(w_pair_t[...], normed.astype(BF16), ((1,), (1,)))
        same = (mine == chain_all[at.r * ROWS + i]).astype(F32)
        strips.append((projected + gain * same).astype(BF16))
    strips = jnp.concatenate(strips, axis=0)
    shape = (HEADS * 16, HEADS * ROWS)
    to, source = iota(shape, 0), iota(shape, 1)
    order = ((to // 16 == source % 16) & (to % 16 == source // 16)).astype(BF16)
    spread = dot(order, strips).astype(BF16)
    for h in range(HEADS):
        rows = spread[h * 16 : (h + 1) * 16]
        bias_send[h, :, :128] = rows[:, :128]
        bias_send[h, :, 128:] = jnp.concatenate([rows[:, 128:], jnp.zeros((16, 64), BF16)], axis=1)


def make_acts(noised, cotangent, gamma, beta, gate, w_query, w_key, w_value, w_out, acts_send):
    noised_norm, _ = norm_rows(noised[...].astype(F32))
    x_b = (noised_norm * gamma + beta).astype(BF16)
    grad_update = (cotangent[...].astype(F32) * gate).astype(BF16)
    arrays = (
        (dot(x_b, w_key[...]), dot(x_b, w_value[...])),
        (dot(x_b, w_query[...]), dot(grad_update, w_out[...], ((1,), (1,)))),
    )
    for part, (first, second) in enumerate(arrays):
        tail = jnp.concatenate([first[128:], second[128:]], axis=0)
        for n, piece in enumerate((first[:128], second[:128], tail)):
            piece = piece.T.astype(BF16)
            for h in range(HEADS):
                acts_send[h, part, n * HEAD : (n + 1) * HEAD, :] = piece[h * HEAD : (h + 1) * HEAD]


def assemble_bias(held):
    strips = []
    for y in range(4):
        parts = [held[y * 4 + b] for b in range(4)]
        tails = [p[:, 128:BLOCK] for p in parts]
        strips.append(jnp.concatenate([p[:, :128] for p in parts] + tails, axis=1))
    strips = jnp.concatenate(strips, axis=0)
    to, source = iota((HEAD, 64), 0), iota((HEAD, 64), 1)
    pick = ((source // 16 == to // ROWS) & (source % 16 == to % ROWS)).astype(BF16)
    return dot(pick, strips).astype(BF16)


def spread_bias(total, to_group):
    to, source = iota((64, HEAD), 0), iota((64, HEAD), 1)
    pick = ((to // 16 == source // ROWS) & (to % 16 == source % ROWS)).astype(BF16)
    spread = dot(pick, total).astype(BF16)
    for y in range(4):
        rows = spread[y * 16 : (y + 1) * 16]
        for b in range(4):
            tail = rows[:, 512 + b * 64 : 512 + (b + 1) * 64]
            to_group[y * 4 + b, :, :128] = rows[:, b * 128 : (b + 1) * 128]
            to_group[y * 4 + b, :, 128:] = jnp.concatenate([tail, jnp.zeros_like(tail)], axis=1)


def half(n):
    return slice(n * 64, n * 64 + 64)


def wide(acts, first, n):
    parts = [acts[first + b, 0, n * HEAD : (n + 1) * HEAD, :] for b in range(4)]
    parts += [acts[first + b, 0, 2 * HEAD :, half(n)] for b in range(4)]
    return jnp.concatenate(parts, axis=1)


def block(acts, place, n):
    return jnp.concatenate(
        [acts[place, 1, n * HEAD : (n + 1) * HEAD, :], acts[place, 1, 2 * HEAD :, half(n)]], axis=1
    )


def attend(query_t, grad_t, key_t, value_t, bias):
    scale = 1.0 / math.sqrt(HEAD)
    query = query_t.astype(F32).T.astype(BF16)
    grad = grad_t.astype(F32).T.astype(BF16)
    scores = dot(query, key_t) * (scale * LOG2E) + bias
    weight = jnp.exp2(scores)
    prob = weight * (1.0 / jnp.sum(weight, axis=-1, keepdims=True))
    grad_prob = dot(grad, value_t)
    scaled = prob * grad_prob
    grad_score = scaled - prob * jnp.sum(scaled, axis=-1, keepdims=True)
    return prob.astype(BF16), grad_score.astype(BF16), grad_score


def thin_rows(spread):
    shape = (16 * 16, BLOCK) if spread else (BLOCK, 16 * 16)
    thin, full = iota(shape, 0 if spread else 1), iota(shape, 1 if spread else 0)
    return ((thin // 16 == full // ROWS) & (thin % 16 == full % ROWS)).astype(BF16)


def back_pieces(grads, part):
    def piece(n):
        rows = [grads[h, part, n * HEAD : (n + 1) * HEAD, :] for h in range(HEADS)]
        return jnp.concatenate(rows, axis=0).astype(F32).T.astype(BF16)

    tail = piece(2)
    return [jnp.concatenate([piece(n), tail[n * 64 : n * 64 + 64]], axis=0) for n in (0, 1)]


def pair_weight(w_pair_t):
    shape = (HEADS * 16, HEADS)
    pick = (iota(shape, 0) // 16 == iota(shape, 1)).astype(BF16)
    return dot(pick, w_pair_t[...]).astype(BF16)


def pair_back(grad_t, weight, pair, result, rows):
    row = iota(weight.shape, 0) % 16
    for i in rows:
        grad = dot(grad_t, jnp.where(row == i, weight, jnp.zeros_like(weight)))
        normed, inverse = norm_rows(pair[i].astype(F32))
        result[i] = norm_back(grad, normed, inverse).astype(BF16)


def block_kernel(
    single_in, pair_in, noised_in, cotangent_in,
    w_gamma_in, w_beta_in, w_outgate_in, w_query_in, w_key_in, w_value_in, w_out_in,
    chain_in, cols_in, gain_in, w_pair_in,
    updated_out, plane_out, d_pair_out,
    single, pair, noised, cotangent, w_gamma, w_beta, w_outgate, w_query, w_key, w_value, w_out,
    bias_send, held, bias_all, acts_send, acts_all, gamma_v, gate_v, bias_f,
    key_t, value_t, grad_key, grad_value,
    to_x, from_x, to_z, from_z, to_group, from_group, grads_send, grads_all,
    part, plane_in, sum_z, own, updated, d_pair, sums_v, inner_v, chain_all, chain_cols, chain_gain, w_pair_t,
    load, sent, got, q_recv, x_recv, u_recv, z_recv,
):
    at = Place()
    barrier = pltpu.get_barrier_semaphore()
    others = [(dx, dy) for dx in (2, 1, 3, 0) for dy in (2, 1, 3, 0) if dx or dy]
    mates = [(dy, c) for dy in (1, 2, 3, 0) for c in (2, 3, 0, 1) if (dy, c) != (0, 0)]
    peers = (
        [at.along("z", k)[1] for k in (2, 1, 3)]
        + [at.same_head(at.far), at.same_head(at.near)]
        + [at.along("x", k)[1] for k in (2, 1, 3)]
        + [at.mate(dy, c)[2] for dy, c in mates]
        + [at.plane(dx, dy)[1] for dx, dy in others if dx and dy]
    )
    loads = {}
    for n, (name, source, target) in enumerate(
        (
            ("chain", chain_in, chain_all),
            ("gain", gain_in, chain_gain),
            ("cols", cols_in, chain_cols),
            ("map", w_pair_in, w_pair_t),
            ("pair", pair_in, pair),
            ("single", single_in, single),
            ("gamma", w_gamma_in, w_gamma),
            ("beta", w_beta_in, w_beta),
            ("gate", w_outgate_in, w_outgate),
            ("noised", noised_in, noised),
            ("query", w_query_in, w_query),
            ("key", w_key_in, w_key),
            ("value", w_value_in, w_value),
            ("cot", cotangent_in, cotangent),
            ("out", w_out_in, w_out),
        )
    ):
        loads[name] = pltpu.make_async_copy(source, target, load.at[n])
        loads[name].start()
        if name == "pair":
            for device in peers:
                pl.semaphore_signal(barrier, inc=1, device_id=device, device_id_type=MESH)

    def send(source, target, ssem, rsem, device):
        remote(source, target, ssem, rsem, device).start()

    def arrive(buffer, rsem):
        remote(buffer, buffer, sent.at[0], rsem, at.along("x", 1)[1]).wait_recv()

    def left(buffer, ssem):
        remote(buffer, buffer, ssem, got.at[0], at.along("x", 1)[1]).wait_send()

    bias_sent, kv_sent, q_sent, z_sent, x_sent, rows_sent, grads_sent = [sent.at[n] for n in range(7)]
    u_sent, near_sent, group_sent, plane_sent, sum_sent, out_sent = [sent.at[n] for n in range(7, 13)]
    bias_got, kv_got, rows_got, grads_got, group_got, plane_got, sum_got, out_got = [
        got.at[n] for n in range(8)
    ]

    for name in ("chain", "gain", "cols", "map", "pair"):
        loads[name].wait()
    pair_bias(pair, chain_cols, chain_all, chain_gain, w_pair_t, at, bias_send)
    pl.semaphore_wait(barrier, len(peers))
    for dy, c in mates:
        _, head, device = at.mate(dy, c)
        send(bias_send.at[head], held.at[at.me], bias_sent, bias_got, device)
    held[at.me] = bias_send[at.head]
    for name in ("single", "gamma", "beta", "gate", "noised", "query", "key", "value", "cot", "out"):
        loads[name].wait()
    single_norm, _ = norm_rows(single[...].astype(F32))
    single_b = single_norm.astype(BF16)
    gamma = jax.nn.sigmoid(dot(single_b, w_gamma[...]))
    beta = dot(single_b, w_beta[...])
    gate = jax.nn.sigmoid(dot(single_b, w_outgate[...]))
    gamma_v[...] = gamma
    gate_v[...] = gate
    make_acts(noised, cotangent, gamma, beta, gate, w_query, w_key, w_value, w_out, acts_send)
    for dy, c in MIXED:
        _, head, device = at.mate(dy, c)
        send(acts_send.at[head, 0], acts_all.at[at.me, 0], kv_sent, kv_got, device)
    acts_all[at.me] = acts_send[at.head]
    arrive(held.at[:15], bias_got)
    bias_all[at.x, at.z] = assemble_bias(held)
    order = (at.z, at.near, at.far, at.opposite)
    rows = bias_all.at[at.x, at.z]
    send(rows, rows, z_sent, z_recv.at[1], at.same_head(at.far))
    send(rows, rows, z_sent, z_recv.at[0], at.same_head(at.near))
    for kz in range(4):
        rows = bias_all.at[at.x, order[kz]]
        if kz:
            arrive(rows, z_recv.at[kz - 1])
        if kz == 2:
            send(rows, rows, z_sent, z_recv.at[2], at.same_head(at.near))
        for k in (2, 1, 3):
            send(rows, rows, x_sent, x_recv.at[k], at.along("x", k)[1])
        if kz == 0:
            for dy, c in MIXED:
                _, head, device = at.mate(dy, c)
                source, target = acts_send.at[head, 1], acts_all.at[at.me, 1]
                send(source, target, q_sent, q_recv.at[dy * 4 + c], device)
    arrive(acts_all.at[:15, 0], kv_got)
    samples = [(at.y + 4 - dy) % 4 for dy in (1, 2, 3, 0)]
    for s, dy in enumerate((1, 2, 3, 0)):
        key_t[s] = wide(acts_all, samples[s] * 4, 0)
        value_t[s] = wide(acts_all, samples[s] * 4, 1)
        grad_key[s] = jnp.zeros((HEAD, TOKENS), F32)
        grad_value[s] = jnp.zeros((HEAD, TOKENS), F32)

    scale = 1.0 / math.sqrt(HEAD)

    def step_body(step, carry):
        k = step + step // 2 - 2 * (step // 3)
        place, device = at.along("x", k)
        c = at.link(place)

        @pl.when(step > 0)
        def _():
            arrive(bias_all.at[place], x_recv.at[4 - k])

        @pl.when(c > 0)
        def _():
            arrive(acts_all.at[at.y * 4 + place, 1], q_recv.at[c])

        for s, dy in enumerate((1, 2, 3)):
            arrive(acts_all.at[samples[s] * 4 + place, 1], q_recv.at[dy * 4 + c])
        for z in range(4):
            bias_f[z * HEAD : (z + 1) * HEAD, :] = bias_all[place, z].astype(F32) * LOG2E

        def weigh(s):
            slot = samples[s] * 4 + place
            query_t = block(acts_all, slot, 0)
            grad_t = block(acts_all, slot, 1)
            return (query_t, grad_t) + attend(query_t, grad_t, key_t[s], value_t[s], bias_f[...])

        ahead = weigh(0)
        total = ahead[4]
        for s, dy in enumerate((1, 2, 3, 0)):
            query_t, grad_t, prob_b, score_b, _ = ahead
            if s < 3:
                ahead = weigh(s + 1)
                total = total + ahead[4]
            slot = samples[s] * 4 + place
            attended = dot(value_t[s], prob_b, ((1,), (1,))).astype(BF16)
            grad_query = (dot(key_t[s], score_b, ((1,), (1,))) * scale).astype(BF16)
            grad_value[s] = grad_value[s] + dot(grad_t, prob_b)
            grad_key[s] = grad_key[s] + dot(query_t, score_b)
            grads_send[slot, 1, :HEAD, :] = attended[:, :128]
            grads_send[slot, 1, HEAD : 2 * HEAD, :] = grad_query[:, :128]
            grads_send[slot, 1, 2 * HEAD :, :64] = attended[:, 128:]
            grads_send[slot, 1, 2 * HEAD :, 64:] = grad_query[:, 128:]
        for z in range(4):
            to_x[k, z] = total[z * HEAD : (z + 1) * HEAD].astype(BF16)

        @pl.when(step > 0)
        def _():
            for kz in (3, 2, 1, 0):
                z = order[kz]
                send(to_x.at[k, z], from_x.at[at.x, z], u_sent, u_recv.at[kz], device)

        for s, dy in enumerate((1, 2, 3, 0)):
            slot = samples[s] * 4 + place
            copy = remote(
                grads_send.at[slot, 1],
                grads_all.at[at.head, 1],
                rows_sent,
                rows_got,
                (at.r - at.y + samples[s], place),
            )
            if dy:
                copy.start()
            else:
                pl.when(c > 0)(copy.start)
        return carry

    lax.fori_loop(0, 4, step_body, 0)
    for s, dy in enumerate((1, 2, 3, 0)):
        key_b = (grad_key[s] * scale).astype(BF16)
        value_b = grad_value[s].astype(BF16)
        for b in range(4):
            slot = samples[s] * 4 + b
            lanes = slice(b * 128, (b + 1) * 128)
            tail = slice(512 + b * 64, 512 + (b + 1) * 64)
            grads_send[slot, 0, :HEAD, :] = key_b[:, lanes]
            grads_send[slot, 0, HEAD : 2 * HEAD, :] = value_b[:, lanes]
            grads_send[slot, 0, 2 * HEAD :, :64] = key_b[:, tail]
            grads_send[slot, 0, 2 * HEAD :, 64:] = value_b[:, tail]
        for c in (2, 0, 3, 1):
            if dy or c:
                slot, _, device = at.mate(4 - dy, c)
                send(grads_send.at[slot, 0], grads_all.at[at.head, 0], grads_sent, grads_got, device)
    grads_all[at.head] = grads_send[at.me]
    from_x[at.x] = to_x[0]
    left(held.at[:15], bias_sent)
    left(acts_all.at[:15, 0], kv_sent)
    left(acts_all.at[:15, 1], q_sent)
    left(bias_all.at[0, :3], z_sent)
    left(bias_all.at[:3], x_sent)
    arrive(grads_all.at[:15, 1], rows_got)
    attended, grad_q = back_pieces(grads_all, 1)
    gamma = gamma_v[...]
    gate = gate_v[...]
    block_update = dot(attended, w_out[...])
    noised_f = noised[...].astype(F32)
    updated[...] = (noised_f + gate * block_update).astype(BF16)
    noised_norm, _ = norm_rows(noised_f)
    back = ((1,), (1,))
    pre_gate = (cotangent[...].astype(F32) * block_update * (gate * (1.0 - gate))).astype(BF16)
    sums_v[...] = dot(pre_gate, w_outgate[...], back)
    inner_v[...] = dot(grad_q, w_query[...], back)
    gamma_v[...] = noised_norm * (gamma * (1.0 - gamma))
    save = pltpu.make_async_copy(updated, updated_out, load.at[0])
    save.start()

    def rows_for(kz):
        z = order[kz]
        arrive(from_x.at[:3, z], u_recv.at[kz])
        rows = from_x[0, z].astype(F32)
        for x in range(1, 4):
            rows = rows + from_x[x, z].astype(F32)
        return rows

    to_z[3] = rows_for(3).astype(BF16)
    send(to_z.at[3], from_z.at[3], near_sent, z_recv.at[5], at.same_head(at.near))
    to_z[1] = rows_for(1).astype(BF16)
    send(to_z.at[1], from_z.at[1], near_sent, z_recv.at[3], at.same_head(at.near))
    arrive(grads_all.at[:15, 0], grads_got)
    grad_k, grad_v = back_pieces(grads_all, 0)
    grad_input = inner_v[...] + dot(grad_k, w_key[...], back) + dot(grad_v, w_value[...], back)
    pre_gamma = (grad_input * gamma_v[...]).astype(BF16)
    sums = sums_v[...] + dot(pre_gamma, w_gamma[...], back)
    sums = sums + dot(grad_input.astype(BF16), w_beta[...], back)
    spread = dot(thin_rows(True), sums.astype(BF16)).astype(BF16)
    for p in range(16):
        part[p] = spread[p * 16 : (p + 1) * 16]
    for dx, dy in others:
        place, device = at.plane(dx, dy)
        send(part.at[place], plane_in.at[at.spot], plane_sent, plane_got, device)
    plane_in[at.spot] = part[at.spot]

    to_far = rows_for(2)
    arrive(from_z.at[3], z_recv.at[5])
    to_z[2] = (to_far + from_z[3].astype(F32)).astype(BF16)
    send(to_z.at[2], from_z.at[2], near_sent, z_recv.at[4], at.same_head(at.far))
    left(grads_all.at[:15, 1], rows_sent)
    left(grads_all.at[:15, 0], grads_sent)
    left(from_x.at[:3], u_sent)
    own_rows = rows_for(0)
    weight = pair_weight(w_pair_t)
    shape = (16, BLOCK)
    mine = iota(shape, 0) + at.spot * ROWS
    pick = ((iota(shape, 1) == mine) & (iota(shape, 0) < ROWS)).astype(BF16)
    normed, inverse = norm_rows(dot(pick, single[...]))
    arrive(plane_in.at[:15], plane_got)
    total = plane_in[0].astype(F32)
    for p in range(1, 16):
        total = total + plane_in[p].astype(F32)
    sum_z[at.z] = total.astype(BF16)
    for k in (2, 1, 3):
        rows = sum_z.at[at.z]
        send(rows, rows, sum_sent, sum_got, at.along("z", k)[1])
    for kz in (1, 2):
        arrive(from_z.at[kz], z_recv.at[2 + kz])
    own_rows = own_rows + from_z[1].astype(F32) + from_z[2].astype(F32)
    spread_bias((own_rows * TOKENS).astype(BF16), to_group)
    for dy, c in mates:
        slot, _, device = at.mate(dy, c)
        send(to_group.at[slot], from_group.at[at.head], group_sent, group_got, device)
    from_group[at.head] = to_group[at.me]
    arrive(sum_z.at[:3], sum_got)
    own[...] = norm_back(total_of(sum_z), normed, inverse).astype(BF16)
    for dx, dy in others:
        send(own, plane_out.at[at.spot], out_sent, out_got, at.plane(dx, dy)[1])
    put = pltpu.make_async_copy(own, plane_out.at[at.spot], load.at[2])
    put.start()
    arrive(from_group.at[:15], group_got)
    grad_t = jnp.concatenate([from_group[h] for h in range(HEADS)], axis=0)
    grad_t = grad_t.astype(F32).T.astype(BF16)[:BLOCK]
    pair_back(grad_t, weight, pair, d_pair, range(ROWS))
    keep = pltpu.make_async_copy(d_pair, d_pair_out, load.at[1])
    keep.start()
    left(from_z.at[:3], near_sent)
    left(plane_in.at[:15], plane_sent)
    left(sum_z.at[:3], sum_sent)
    left(from_group.at[:15], group_sent)
    save.wait()
    keep.wait()
    put.wait()
    left(plane_in.at[:15], out_sent)
    arrive(plane_out.at[:15], out_got)


def finish_kernel(*refs):
    sources, results, held, sums, sems = refs[:3], refs[3:6], refs[6:9], refs[9], refs[10]
    loads = [pltpu.make_async_copy(sources[n], held[n], sems.at[n]) for n in range(3)]
    ready = (held[0], sums, held[2])
    stores = [pltpu.make_async_copy(ready[n], results[n], sems.at[3 + n]) for n in range(3)]
    for copy in loads:
        copy.start()
    pick = thin_rows(False)
    for n in range(3):
        loads[n].wait()
        if n == 1:
            sums[...] = dot(pick, jnp.concatenate([held[1][p] for p in range(16)], axis=0))
        stores[n].start()
    for copy in stores:
        copy.wait()


def on_device(
    single,
    pair,
    chains,
    noised,
    w_gamma,
    w_beta,
    w_outgate,
    w_query,
    w_key,
    w_value,
    w_out,
    w_pair,
    chain_gain,
    cotangent,
):
    def space(*shape):
        return pltpu.VMEM(shape, BF16)

    def wide_space(*shape):
        return pltpu.VMEM(shape, F32)

    def dma(count):
        return pltpu.SemaphoreType.DMA((count,))

    half_width = WIDTH // 2
    results = pl.pallas_call(
        block_kernel,
        out_shape=[
            jax.ShapeDtypeStruct((BLOCK, WIDTH), BF16),
            jax.ShapeDtypeStruct((16, 16, half_width), BF16),
            jax.ShapeDtypeStruct(pair.shape, BF16),
        ],
        in_specs=[ANY] * 15,
        out_specs=[ANY] * 3,
        scratch_shapes=[
            space(BLOCK, half_width),
            space(ROWS, BLOCK, 128),
            space(BLOCK, WIDTH),
            space(BLOCK, WIDTH),
        ]
        + [space(half_width, WIDTH)] * 3
        + [space(WIDTH, WIDTH)] * 4
        + [
            space(16, 16, 256),
            space(16, 16, 256),
            space(4, 4, HEAD, TOKENS),
            space(16, 2, CHUNK, 128),
            space(16, 2, CHUNK, 128),
            wide_space(BLOCK, WIDTH),
            wide_space(BLOCK, WIDTH),
            wide_space(BLOCK, TOKENS),
            space(4, HEAD, TOKENS),
            space(4, HEAD, TOKENS),
            wide_space(4, HEAD, TOKENS),
            wide_space(4, HEAD, TOKENS),
            space(4, 4, HEAD, TOKENS),
            space(4, 4, HEAD, TOKENS),
            space(4, HEAD, TOKENS),
            space(4, HEAD, TOKENS),
            space(16, 16, 256),
            space(16, 16, 256),
            space(16, 2, CHUNK, 128),
            space(16, 2, CHUNK, 128),
        ]
        + [
            space(16, 16, half_width),
            space(16, 16, half_width),
            space(4, 16, half_width),
            space(16, half_width),
        ]
        + [space(BLOCK, WIDTH), space(ROWS, BLOCK, 128)]
        + [wide_space(BLOCK, half_width), wide_space(BLOCK, WIDTH)]
        + [
            pltpu.SMEM((TOKENS,), jnp.int32),
            pltpu.VMEM((1, TOKENS), jnp.int32),
            pltpu.SMEM((HEADS,), F32),
            space(HEADS, 128),
        ]
        + [dma(15), dma(13), dma(8), dma(16), dma(4), dma(4), dma(6)],
        compiler_params=pltpu.CompilerParams(
            vmem_limit_bytes=VMEM_BYTES, collective_id=0, has_side_effects=True
        ),
        name="block",
    )(
        single,
        pair,
        noised.reshape(BLOCK, WIDTH),
        cotangent.reshape(BLOCK, WIDTH),
        w_gamma,
        w_beta,
        w_outgate,
        w_query,
        w_key,
        w_value,
        w_out,
        chains,
        chains.reshape(1, TOKENS),
        chain_gain,
        w_pair.T,
    )
    updated, d_single, d_pair = pl.pallas_call(
        finish_kernel,
        out_shape=[
            jax.ShapeDtypeStruct((BLOCK, WIDTH), BF16),
            jax.ShapeDtypeStruct((BLOCK, half_width), F32),
            jax.ShapeDtypeStruct(pair.shape, BF16),
        ],
        in_specs=[ANY] * 3,
        out_specs=[ANY] * 3,
        scratch_shapes=[
            space(BLOCK, WIDTH),
            space(16, 16, half_width),
            space(*pair.shape),
            wide_space(BLOCK, half_width),
            dma(6),
        ],
        compiler_params=pltpu.CompilerParams(vmem_limit_bytes=VMEM_BYTES),
        name="finish",
    )(*results)
    return updated.reshape(1, BLOCK, WIDTH), d_single, d_pair


def solution(mesh):
    rows = P("rows", "grp", None)
    grp = P("grp", None)
    in_specs = (grp, rows, P(), rows) + (P(),) * 9 + (rows,)
    return jax.shard_map(
        on_device, mesh=mesh, in_specs=in_specs, out_specs=(rows, grp, rows), check_vma=False
    )
```

```python
import math

import jax
import jax.numpy as jnp
from jax import lax
from jax.experimental import pallas as pl
from jax.experimental.pallas import tpu as pltpu
from jax.sharding import PartitionSpec as P

EPSILON = 1e-05
LOG2E = math.log2(math.e)
F32 = jnp.float32
BF16 = jnp.bfloat16
MESH = pl.DeviceIdType.MESH
ANY = pl.BlockSpec(memory_space=pl.ANY)
VMEM = pl.BlockSpec(memory_space=pltpu.VMEM)
SMEM = pl.BlockSpec(memory_space=pltpu.SMEM)
VMEM_BYTES = 56 * 1024 * 1024

HEADS = 16
HEAD = 48
WIDTH = 768
TOKENS = 768
BLOCK = 192
ROWS = 12
CHUNK = 3 * HEAD


MIXED = (
    (1, 2), (3, 0), (2, 2), (1, 0), (3, 2), (2, 0), (0, 2), (0, 1),
    (1, 3), (3, 1), (2, 3), (1, 1), (3, 3), (2, 1), (0, 3),
)


def dot(left, right, contract=((1,), (0,))):
    return lax.dot_general(left, right, (contract, ((), ())), preferred_element_type=F32)


def norm_rows(values):
    center = values - jnp.mean(values, axis=-1, keepdims=True)
    inverse = lax.rsqrt(jnp.mean(center * center, axis=-1, keepdims=True) + EPSILON)
    return center * inverse, inverse


def norm_back(grad_in, normed, inverse):
    grad_mean = jnp.mean(grad_in, axis=-1, keepdims=True)
    cross_mean = jnp.mean(grad_in * normed, axis=-1, keepdims=True)
    return inverse * (grad_in - grad_mean - normed * cross_mean)


def iota(shape, dim):
    return lax.broadcasted_iota(jnp.int32, shape, dim)


class Place:
    def __init__(self):
        self.r = lax.axis_index("rows")
        self.b = lax.axis_index("grp")
        self.x = self.r // 16
        self.z = (self.r // 4) % 4
        self.y = self.r % 4
        self.spot = self.x * 4 + self.y
        self.me = self.y * 4 + self.b
        self.flip = 2 * (self.z % 2)
        self.head = self.y * 4 + (self.b + self.flip) % 4
        toward = 2 * (self.b // 2) - 1
        self.near = (self.z + 4 + toward) % 4
        self.far = (self.z + 4 - toward) % 4
        self.opposite = (self.z + 2) % 4

    def mate(self, dy, c):
        y = (self.y + dy) % 4
        b = (self.b + 2 * (c // 2)) % 4
        if c % 2:
            b = b + 1 - 2 * (b % 2)
        head = y * 4 + (b + self.flip) % 4
        return y * 4 + b, head, (self.r - self.y + y, b)

    def link(self, b):
        return 2 * ((self.b // 2 + b // 2) % 2) + (self.b + b) % 2

    def same_head(self, z):
        return (self.r + (z - self.z) * 4, (self.b + 2) % 4)

    def plane(self, dx, dy):
        x, y = (self.x + dx) % 4, (self.y + dy) % 4
        return x * 4 + y, (self.r + (x - self.x) * 16 + (y - self.y), self.b)

    def along(self, axis, k):
        if axis == "x":
            place = (self.x + k) % 4
            return place, (self.r + (place - self.x) * 16, self.b)
        if axis == "z":
            place = (self.z + k) % 4
            return place, (self.r + (place - self.z) * 4, self.b)
        place = (self.y + k) % 4
        return place, (self.r + (place - self.y), self.b)

    def along_from(self, axis, k):
        return ({"x": self.x, "z": self.z, "y": self.y}[axis] + 4 - k) % 4


def remote(source, target, send, recv, device):
    return pltpu.make_async_remote_copy(
        src_ref=source,
        dst_ref=target,
        send_sem=send,
        recv_sem=recv,
        device_id=device,
        device_id_type=MESH,
    )


def total_of(ref, rows=slice(None)):
    value = ref[0, rows, :].astype(F32)
    for n in range(1, 4):
        value = value + ref[n, rows, :].astype(F32)
    return value


def pair_bias(pair, chain_cols, chain_all, chain_gain, w_pair_t, at, bias_send):
    cols = chain_cols[...]
    mine = cols[:, :BLOCK]
    for b in range(1, 4):
        mine = jnp.where(at.b == b, cols[:, b * BLOCK : (b + 1) * BLOCK], mine)
    head = iota((HEADS, 1), 0)
    gain = jnp.zeros((HEADS, 1), F32)
    for h in range(HEADS):
        gain = jnp.where(head == h, chain_gain[h], gain)
    strips = []
    for i in range(ROWS):
        normed, _ = norm_rows(pair[i].astype(F32))
        projected = dot(w_pair_t[...], normed.astype(BF16), ((1,), (1,)))
        same = (mine == chain_all[at.r * ROWS + i]).astype(F32)
        strips.append((projected + gain * same).astype(BF16))
    strips = jnp.concatenate(strips, axis=0)
    shape = (HEADS * 16, HEADS * ROWS)
    to, source = iota(shape, 0), iota(shape, 1)
    order = ((to // 16 == source % 16) & (to % 16 == source // 16)).astype(BF16)
    spread = dot(order, strips).astype(BF16)
    for h in range(HEADS):
        rows = spread[h * 16 : (h + 1) * 16]
        bias_send[h, :, :128] = rows[:, :128]
        bias_send[h, :, 128:] = jnp.concatenate([rows[:, 128:], jnp.zeros((16, 64), BF16)], axis=1)


def put_acts(part, first, second, acts_send):
    tail = jnp.concatenate([first[128:], second[128:]], axis=0)
    for n, piece in enumerate((first[:128], second[:128], tail)):
        piece = piece.T.astype(BF16)
        for h in range(HEADS):
            acts_send[h, part, n * HEAD : (n + 1) * HEAD, :] = piece[h * HEAD : (h + 1) * HEAD]


def assemble_bias(held):
    strips = []
    for y in range(4):
        parts = [held[y * 4 + b] for b in range(4)]
        tails = [p[:, 128:BLOCK] for p in parts]
        strips.append(jnp.concatenate([p[:, :128] for p in parts] + tails, axis=1))
    strips = jnp.concatenate(strips, axis=0)
    to, source = iota((HEAD, 64), 0), iota((HEAD, 64), 1)
    pick = ((source // 16 == to // ROWS) & (source % 16 == to % ROWS)).astype(BF16)
    return dot(pick, strips).astype(BF16)


def spread_bias(total, to_group):
    to, source = iota((64, HEAD), 0), iota((64, HEAD), 1)
    pick = ((to // 16 == source // ROWS) & (to % 16 == source % ROWS)).astype(BF16)
    spread = dot(pick, total).astype(BF16)
    for y in range(4):
        rows = spread[y * 16 : (y + 1) * 16]
        for b in range(4):
            tail = rows[:, 512 + b * 64 : 512 + (b + 1) * 64]
            to_group[y * 4 + b, :, :128] = rows[:, b * 128 : (b + 1) * 128]
            to_group[y * 4 + b, :, 128:] = jnp.concatenate([tail, jnp.zeros_like(tail)], axis=1)


def half(n):
    return slice(n * 64, n * 64 + 64)


def wide(acts, first, n):
    parts = [acts[first + b, 0, n * HEAD : (n + 1) * HEAD, :] for b in range(4)]
    parts += [acts[first + b, 0, 2 * HEAD :, half(n)] for b in range(4)]
    return jnp.concatenate(parts, axis=1)


def block(acts, place, n):
    return jnp.concatenate(
        [acts[place, 1, n * HEAD : (n + 1) * HEAD, :], acts[place, 1, 2 * HEAD :, half(n)]], axis=1
    )


def attend(query_t, grad_t, key_t, value_t, bias):
    scale = 1.0 / math.sqrt(HEAD)
    query = query_t.astype(F32).T.astype(BF16)
    grad = grad_t.astype(F32).T.astype(BF16)
    scores = dot(query, key_t) * (scale * LOG2E) + bias
    weight = jnp.exp2(scores)
    prob = weight * (1.0 / jnp.sum(weight, axis=-1, keepdims=True))
    grad_prob = dot(grad, value_t)
    scaled = prob * grad_prob
    grad_score = scaled - prob * jnp.sum(scaled, axis=-1, keepdims=True)
    return prob.astype(BF16), grad_score.astype(BF16), grad_score


def thin_rows(spread):
    shape = (16 * 16, BLOCK) if spread else (BLOCK, 16 * 16)
    thin, full = iota(shape, 0 if spread else 1), iota(shape, 1 if spread else 0)
    return ((thin // 16 == full // ROWS) & (thin % 16 == full % ROWS)).astype(BF16)


def back_pieces(grads, part):
    def piece(n):
        rows = [grads[h, part, n * HEAD : (n + 1) * HEAD, :] for h in range(HEADS)]
        return jnp.concatenate(rows, axis=0).astype(F32).T.astype(BF16)

    tail = piece(2)
    return [jnp.concatenate([piece(n), tail[n * 64 : n * 64 + 64]], axis=0) for n in (0, 1)]


def pair_weight(w_pair_t):
    shape = (HEADS * 16, HEADS)
    pick = (iota(shape, 0) // 16 == iota(shape, 1)).astype(BF16)
    return dot(pick, w_pair_t[...]).astype(BF16)


def pair_back(grad_t, weight, pair, result, rows):
    row = iota(weight.shape, 0) % 16
    for i in rows:
        grad = dot(grad_t, jnp.where(row == i, weight, jnp.zeros_like(weight)))
        normed, inverse = norm_rows(pair[i].astype(F32))
        result[i] = norm_back(grad, normed, inverse).astype(BF16)


def block_kernel(
    single_in, pair_in, noised_in, cotangent_in,
    w_gamma_in, w_beta_in, w_outgate_in, w_query_in, w_key_in, w_value_in, w_out_in,
    chain_in, cols_in, gain_in, w_pair_in,
    updated_out, plane_out, d_pair_out,
    single, pair, noised, cotangent, w_gamma, w_beta, w_outgate, w_query, w_key, w_value, w_out,
    bias_send, held, bias_all, acts_send, acts_all, gamma_v, gate_v, bias_f,
    key_t, value_t, grad_key, grad_value,
    to_x, from_x, to_z, from_z, to_group, from_group, grads_send, grads_all,
    part, plane_in, sum_z, own, updated, d_pair, sums_v, inner_v, chain_all, chain_cols, chain_gain, w_pair_t,
    load, sent, got, q_recv, x_recv, u_recv, z_recv,
):
    at = Place()
    barrier = pltpu.get_barrier_semaphore()
    others = [(dx, dy) for dx in (2, 1, 3, 0) for dy in (2, 1, 3, 0) if dx or dy]
    mates = [(dy, c) for dy in (1, 2, 3, 0) for c in (2, 3, 0, 1) if (dy, c) != (0, 0)]
    peers = (
        [at.along("z", k)[1] for k in (2, 1, 3)]
        + [at.same_head(at.far), at.same_head(at.near)]
        + [at.along("x", k)[1] for k in (2, 1, 3)]
        + [at.mate(dy, c)[2] for dy, c in mates]
        + [at.plane(dx, dy)[1] for dx, dy in others if dx and dy]
    )
    loads = {}
    for n, (name, source, target) in enumerate(
        (
            ("chain", chain_in, chain_all),
            ("gain", gain_in, chain_gain),
            ("cols", cols_in, chain_cols),
            ("map", w_pair_in, w_pair_t),
            ("pair", pair_in, pair),
            ("single", single_in, single),
            ("gamma", w_gamma_in, w_gamma),
            ("beta", w_beta_in, w_beta),
            ("noised", noised_in, noised),
            ("key", w_key_in, w_key),
            ("value", w_value_in, w_value),
            ("gate", w_outgate_in, w_outgate),
            ("cot", cotangent_in, cotangent),
            ("out", w_out_in, w_out),
            ("query", w_query_in, w_query),
        )
    ):
        loads[name] = pltpu.make_async_copy(source, target, load.at[n])
        loads[name].start()
        if name == "pair":
            for device in peers:
                pl.semaphore_signal(barrier, inc=1, device_id=device, device_id_type=MESH)

    def send(source, target, ssem, rsem, device):
        remote(source, target, ssem, rsem, device).start()

    def arrive(buffer, rsem):
        remote(buffer, buffer, sent.at[0], rsem, at.along("x", 1)[1]).wait_recv()

    def left(buffer, ssem):
        remote(buffer, buffer, ssem, got.at[0], at.along("x", 1)[1]).wait_send()

    bias_sent, kv_sent, q_sent, z_sent, x_sent, rows_sent, grads_sent = [sent.at[n] for n in range(7)]
    u_sent, near_sent, group_sent, plane_sent, sum_sent, out_sent = [sent.at[n] for n in range(7, 13)]
    bias_got, kv_got, rows_got, grads_got, group_got, plane_got, sum_got, out_got = [
        got.at[n] for n in range(8)
    ]

    for name in ("chain", "gain", "cols", "map", "pair"):
        loads[name].wait()
    pair_bias(pair, chain_cols, chain_all, chain_gain, w_pair_t, at, bias_send)
    pl.semaphore_wait(barrier, len(peers))
    for dy, c in mates:
        _, head, device = at.mate(dy, c)
        send(bias_send.at[head], held.at[at.me], bias_sent, bias_got, device)
    held[at.me] = bias_send[at.head]
    def send_kv(mates):
        for dy, c in mates:
            _, head, device = at.mate(dy, c)
            send(acts_send.at[head, 0], acts_all.at[at.me, 0], kv_sent, kv_got, device)

    for name in ("single", "gamma", "beta", "noised", "key", "value"):
        loads[name].wait()
    single_norm, _ = norm_rows(single[...].astype(F32))
    single_b = single_norm.astype(BF16)
    gamma = jax.nn.sigmoid(dot(single_b, w_gamma[...]))
    beta = dot(single_b, w_beta[...])
    gamma_v[...] = gamma
    noised_norm, _ = norm_rows(noised[...].astype(F32))
    x_b = (noised_norm * gamma + beta).astype(BF16)
    put_acts(0, dot(x_b, w_key[...]), dot(x_b, w_value[...]), acts_send)
    send_kv(MIXED[:8])
    for name in ("gate", "cot", "out", "query"):
        loads[name].wait()
    gate = jax.nn.sigmoid(dot(single_b, w_outgate[...]))
    gate_v[...] = gate
    grad_update = (cotangent[...].astype(F32) * gate).astype(BF16)
    grad_attn = dot(grad_update, w_out[...], ((1,), (1,)))
    put_acts(1, dot(x_b, w_query[...]), grad_attn, acts_send)
    acts_all[at.me] = acts_send[at.head]
    arrive(held.at[:15], bias_got)
    bias_all[at.x, at.z] = assemble_bias(held)
    order = (at.z, at.near, at.far, at.opposite)
    rows = bias_all.at[at.x, at.z]
    send(rows, rows, z_sent, z_recv.at[1], at.same_head(at.far))
    send(rows, rows, z_sent, z_recv.at[0], at.same_head(at.near))
    send_kv(MIXED[8:])
    for kz in range(4):
        rows = bias_all.at[at.x, order[kz]]
        if kz:
            arrive(rows, z_recv.at[kz - 1])
        if kz == 2:
            send(rows, rows, z_sent, z_recv.at[2], at.same_head(at.near))
        for k in (2, 1, 3):
            send(rows, rows, x_sent, x_recv.at[k], at.along("x", k)[1])
        if kz == 0:
            for dy, c in MIXED:
                _, head, device = at.mate(dy, c)
                source, target = acts_send.at[head, 1], acts_all.at[at.me, 1]
                send(source, target, q_sent, q_recv.at[dy * 4 + c], device)
    arrive(acts_all.at[:15, 0], kv_got)
    samples = [(at.y + 4 - dy) % 4 for dy in (1, 2, 3, 0)]
    for s, dy in enumerate((1, 2, 3, 0)):
        key_t[s] = wide(acts_all, samples[s] * 4, 0)
        value_t[s] = wide(acts_all, samples[s] * 4, 1)
        grad_key[s] = jnp.zeros((HEAD, TOKENS), F32)
        grad_value[s] = jnp.zeros((HEAD, TOKENS), F32)

    scale = 1.0 / math.sqrt(HEAD)

    def step_body(step, carry):
        k = step + step // 2 - 2 * (step // 3)
        place, device = at.along("x", k)
        c = at.link(place)

        @pl.when(step > 0)
        def _():
            arrive(bias_all.at[place], x_recv.at[4 - k])

        @pl.when(c > 0)
        def _():
            arrive(acts_all.at[at.y * 4 + place, 1], q_recv.at[c])

        for s, dy in enumerate((1, 2, 3)):
            arrive(acts_all.at[samples[s] * 4 + place, 1], q_recv.at[dy * 4 + c])
        for z in range(4):
            bias_f[z * HEAD : (z + 1) * HEAD, :] = bias_all[place, z].astype(F32) * LOG2E

        def weigh(s):
            slot = samples[s] * 4 + place
            query_t = block(acts_all, slot, 0)
            grad_t = block(acts_all, slot, 1)
            return (query_t, grad_t) + attend(query_t, grad_t, key_t[s], value_t[s], bias_f[...])

        ahead = weigh(0)
        total = ahead[4]
        for s, dy in enumerate((1, 2, 3, 0)):
            query_t, grad_t, prob_b, score_b, _ = ahead
            if s < 3:
                ahead = weigh(s + 1)
                total = total + ahead[4]
            slot = samples[s] * 4 + place
            attended = dot(value_t[s], prob_b, ((1,), (1,))).astype(BF16)
            grad_query = (dot(key_t[s], score_b, ((1,), (1,))) * scale).astype(BF16)
            grad_value[s] = grad_value[s] + dot(grad_t, prob_b)
            grad_key[s] = grad_key[s] + dot(query_t, score_b)
            grads_send[slot, 1, :HEAD, :] = attended[:, :128]
            grads_send[slot, 1, HEAD : 2 * HEAD, :] = grad_query[:, :128]
            grads_send[slot, 1, 2 * HEAD :, :64] = attended[:, 128:]
            grads_send[slot, 1, 2 * HEAD :, 64:] = grad_query[:, 128:]
        for z in range(4):
            to_x[k, z] = total[z * HEAD : (z + 1) * HEAD].astype(BF16)

        @pl.when(step > 0)
        def _():
            for kz in (3, 2, 1, 0):
                z = order[kz]
                send(to_x.at[k, z], from_x.at[at.x, z], u_sent, u_recv.at[kz], device)

        for s, dy in enumerate((1, 2, 3, 0)):
            slot = samples[s] * 4 + place
            copy = remote(
                grads_send.at[slot, 1],
                grads_all.at[at.head, 1],
                rows_sent,
                rows_got,
                (at.r - at.y + samples[s], place),
            )
            if dy:
                copy.start()
            else:
                pl.when(c > 0)(copy.start)
        return carry

    lax.fori_loop(0, 4, step_body, 0)
    for s, dy in enumerate((1, 2, 3, 0)):
        key_b = (grad_key[s] * scale).astype(BF16)
        value_b = grad_value[s].astype(BF16)
        for b in range(4):
            slot = samples[s] * 4 + b
            lanes = slice(b * 128, (b + 1) * 128)
            tail = slice(512 + b * 64, 512 + (b + 1) * 64)
            grads_send[slot, 0, :HEAD, :] = key_b[:, lanes]
            grads_send[slot, 0, HEAD : 2 * HEAD, :] = value_b[:, lanes]
            grads_send[slot, 0, 2 * HEAD :, :64] = key_b[:, tail]
            grads_send[slot, 0, 2 * HEAD :, 64:] = value_b[:, tail]
        for c in (2, 0, 3, 1):
            if dy or c:
                slot, _, device = at.mate(4 - dy, c)
                send(grads_send.at[slot, 0], grads_all.at[at.head, 0], grads_sent, grads_got, device)
    grads_all[at.head] = grads_send[at.me]
    from_x[at.x] = to_x[0]
    left(held.at[:15], bias_sent)
    left(acts_all.at[:15, 0], kv_sent)
    left(acts_all.at[:15, 1], q_sent)
    left(bias_all.at[0, :3], z_sent)
    left(bias_all.at[:3], x_sent)
    arrive(grads_all.at[:15, 1], rows_got)
    attended, grad_q = back_pieces(grads_all, 1)
    gamma = gamma_v[...]
    gate = gate_v[...]
    block_update = dot(attended, w_out[...])
    noised_f = noised[...].astype(F32)
    updated[...] = (noised_f + gate * block_update).astype(BF16)
    noised_norm, _ = norm_rows(noised_f)
    back = ((1,), (1,))
    pre_gate = (cotangent[...].astype(F32) * block_update * (gate * (1.0 - gate))).astype(BF16)
    sums_v[...] = dot(pre_gate, w_outgate[...], back)
    inner_v[...] = dot(grad_q, w_query[...], back)
    gamma_v[...] = noised_norm * (gamma * (1.0 - gamma))
    save = pltpu.make_async_copy(updated, updated_out, load.at[0])
    save.start()

    def rows_for(kz):
        z = order[kz]
        arrive(from_x.at[:3, z], u_recv.at[kz])
        rows = from_x[0, z].astype(F32)
        for x in range(1, 4):
            rows = rows + from_x[x, z].astype(F32)
        return rows

    to_z[3] = rows_for(3).astype(BF16)
    send(to_z.at[3], from_z.at[3], near_sent, z_recv.at[5], at.same_head(at.near))
    to_z[1] = rows_for(1).astype(BF16)
    send(to_z.at[1], from_z.at[1], near_sent, z_recv.at[3], at.same_head(at.near))
    arrive(grads_all.at[:15, 0], grads_got)
    grad_k, grad_v = back_pieces(grads_all, 0)
    grad_input = inner_v[...] + dot(grad_k, w_key[...], back) + dot(grad_v, w_value[...], back)
    pre_gamma = (grad_input * gamma_v[...]).astype(BF16)
    sums = sums_v[...] + dot(pre_gamma, w_gamma[...], back)
    sums = sums + dot(grad_input.astype(BF16), w_beta[...], back)
    spread = dot(thin_rows(True), sums.astype(BF16)).astype(BF16)
    for p in range(16):
        part[p] = spread[p * 16 : (p + 1) * 16]
    for dx, dy in others:
        place, device = at.plane(dx, dy)
        send(part.at[place], plane_in.at[at.spot], plane_sent, plane_got, device)
    plane_in[at.spot] = part[at.spot]

    to_far = rows_for(2)
    arrive(from_z.at[3], z_recv.at[5])
    to_z[2] = (to_far + from_z[3].astype(F32)).astype(BF16)
    send(to_z.at[2], from_z.at[2], near_sent, z_recv.at[4], at.same_head(at.far))
    left(grads_all.at[:15, 1], rows_sent)
    left(grads_all.at[:15, 0], grads_sent)
    left(from_x.at[:3], u_sent)
    own_rows = rows_for(0)
    weight = pair_weight(w_pair_t)
    shape = (16, BLOCK)
    mine = iota(shape, 0) + at.spot * ROWS
    pick = ((iota(shape, 1) == mine) & (iota(shape, 0) < ROWS)).astype(BF16)
    normed, inverse = norm_rows(dot(pick, single[...]))
    arrive(plane_in.at[:15], plane_got)
    total = plane_in[0].astype(F32)
    for p in range(1, 16):
        total = total + plane_in[p].astype(F32)
    sum_z[at.z] = total.astype(BF16)
    for k in (2, 1, 3):
        rows = sum_z.at[at.z]
        send(rows, rows, sum_sent, sum_got, at.along("z", k)[1])
    for kz in (1, 2):
        arrive(from_z.at[kz], z_recv.at[2 + kz])
    own_rows = own_rows + from_z[1].astype(F32) + from_z[2].astype(F32)
    spread_bias((own_rows * TOKENS).astype(BF16), to_group)
    for dy, c in mates:
        slot, _, device = at.mate(dy, c)
        send(to_group.at[slot], from_group.at[at.head], group_sent, group_got, device)
    from_group[at.head] = to_group[at.me]
    arrive(sum_z.at[:3], sum_got)
    own[...] = norm_back(total_of(sum_z), normed, inverse).astype(BF16)
    for dx, dy in others:
        send(own, plane_out.at[at.spot], out_sent, out_got, at.plane(dx, dy)[1])
    put = pltpu.make_async_copy(own, plane_out.at[at.spot], load.at[2])
    put.start()
    arrive(from_group.at[:15], group_got)
    grad_t = jnp.concatenate([from_group[h] for h in range(HEADS)], axis=0)
    grad_t = grad_t.astype(F32).T.astype(BF16)[:BLOCK]
    pair_back(grad_t, weight, pair, d_pair, range(ROWS))
    keep = pltpu.make_async_copy(d_pair, d_pair_out, load.at[1])
    keep.start()
    left(from_z.at[:3], near_sent)
    left(plane_in.at[:15], plane_sent)
    left(sum_z.at[:3], sum_sent)
    left(from_group.at[:15], group_sent)
    save.wait()
    keep.wait()
    put.wait()
    left(plane_in.at[:15], out_sent)
    arrive(plane_out.at[:15], out_got)


def finish_kernel(*refs):
    sources, results, held, sums, sems = refs[:3], refs[3:6], refs[6:9], refs[9], refs[10]
    loads = [pltpu.make_async_copy(sources[n], held[n], sems.at[n]) for n in range(3)]
    ready = (held[0], sums, held[2])
    stores = [pltpu.make_async_copy(ready[n], results[n], sems.at[3 + n]) for n in range(3)]
    for copy in loads:
        copy.start()
    pick = thin_rows(False)
    for n in range(3):
        loads[n].wait()
        if n == 1:
            sums[...] = dot(pick, jnp.concatenate([held[1][p] for p in range(16)], axis=0))
        stores[n].start()
    for copy in stores:
        copy.wait()


def on_device(
    single,
    pair,
    chains,
    noised,
    w_gamma,
    w_beta,
    w_outgate,
    w_query,
    w_key,
    w_value,
    w_out,
    w_pair,
    chain_gain,
    cotangent,
):
    def space(*shape):
        return pltpu.VMEM(shape, BF16)

    def wide_space(*shape):
        return pltpu.VMEM(shape, F32)

    def dma(count):
        return pltpu.SemaphoreType.DMA((count,))

    half_width = WIDTH // 2
    results = pl.pallas_call(
        block_kernel,
        out_shape=[
            jax.ShapeDtypeStruct((BLOCK, WIDTH), BF16),
            jax.ShapeDtypeStruct((16, 16, half_width), BF16),
            jax.ShapeDtypeStruct(pair.shape, BF16),
        ],
        in_specs=[ANY] * 15,
        out_specs=[ANY] * 3,
        scratch_shapes=[
            space(BLOCK, half_width),
            space(ROWS, BLOCK, 128),
            space(BLOCK, WIDTH),
            space(BLOCK, WIDTH),
        ]
        + [space(half_width, WIDTH)] * 3
        + [space(WIDTH, WIDTH)] * 4
        + [
            space(16, 16, 256),
            space(16, 16, 256),
            space(4, 4, HEAD, TOKENS),
            space(16, 2, CHUNK, 128),
            space(16, 2, CHUNK, 128),
            wide_space(BLOCK, WIDTH),
            wide_space(BLOCK, WIDTH),
            wide_space(BLOCK, TOKENS),
            space(4, HEAD, TOKENS),
            space(4, HEAD, TOKENS),
            wide_space(4, HEAD, TOKENS),
            wide_space(4, HEAD, TOKENS),
            space(4, 4, HEAD, TOKENS),
            space(4, 4, HEAD, TOKENS),
            space(4, HEAD, TOKENS),
            space(4, HEAD, TOKENS),
            space(16, 16, 256),
            space(16, 16, 256),
            space(16, 2, CHUNK, 128),
            space(16, 2, CHUNK, 128),
        ]
        + [
            space(16, 16, half_width),
            space(16, 16, half_width),
            space(4, 16, half_width),
            space(16, half_width),
        ]
        + [space(BLOCK, WIDTH), space(ROWS, BLOCK, 128)]
        + [wide_space(BLOCK, half_width), wide_space(BLOCK, WIDTH)]
        + [
            pltpu.SMEM((TOKENS,), jnp.int32),
            pltpu.VMEM((1, TOKENS), jnp.int32),
            pltpu.SMEM((HEADS,), F32),
            space(HEADS, 128),
        ]
        + [dma(15), dma(13), dma(8), dma(16), dma(4), dma(4), dma(6)],
        compiler_params=pltpu.CompilerParams(
            vmem_limit_bytes=VMEM_BYTES, collective_id=0, has_side_effects=True
        ),
        name="block",
    )(
        single,
        pair,
        noised.reshape(BLOCK, WIDTH),
        cotangent.reshape(BLOCK, WIDTH),
        w_gamma,
        w_beta,
        w_outgate,
        w_query,
        w_key,
        w_value,
        w_out,
        chains,
        chains.reshape(1, TOKENS),
        chain_gain,
        w_pair.T,
    )
    updated, d_single, d_pair = pl.pallas_call(
        finish_kernel,
        out_shape=[
            jax.ShapeDtypeStruct((BLOCK, WIDTH), BF16),
            jax.ShapeDtypeStruct((BLOCK, half_width), F32),
            jax.ShapeDtypeStruct(pair.shape, BF16),
        ],
        in_specs=[ANY] * 3,
        out_specs=[ANY] * 3,
        scratch_shapes=[
            space(BLOCK, WIDTH),
            space(16, 16, half_width),
            space(*pair.shape),
            wide_space(BLOCK, half_width),
            dma(6),
        ],
        compiler_params=pltpu.CompilerParams(vmem_limit_bytes=VMEM_BYTES),
        name="finish",
    )(*results)
    return updated.reshape(1, BLOCK, WIDTH), d_single, d_pair


def solution(mesh):
    rows = P("rows", "grp", None)
    grp = P("grp", None)
    in_specs = (grp, rows, P(), rows) + (P(),) * 9 + (rows,)
    return jax.shard_map(
        on_device, mesh=mesh, in_specs=in_specs, out_specs=(rows, grp, rows), check_vma=False
    )
```

```python
import math

import jax
import jax.numpy as jnp
from jax import lax
from jax.experimental import pallas as pl
from jax.experimental.pallas import tpu as pltpu
from jax.sharding import PartitionSpec as P

EPSILON = 1e-05
LOG2E = math.log2(math.e)
F32 = jnp.float32
BF16 = jnp.bfloat16
MESH = pl.DeviceIdType.MESH
ANY = pl.BlockSpec(memory_space=pl.ANY)
VMEM = pl.BlockSpec(memory_space=pltpu.VMEM)
SMEM = pl.BlockSpec(memory_space=pltpu.SMEM)
VMEM_BYTES = 56 * 1024 * 1024

HEADS = 16
HEAD = 48
WIDTH = 768
TOKENS = 768
BLOCK = 192
ROWS = 12
CHUNK = 3 * HEAD


MIXED = (
    (1, 2), (3, 0), (2, 2), (1, 0), (3, 2), (2, 0), (0, 2), (0, 1),
    (1, 3), (3, 1), (2, 3), (1, 1), (3, 3), (2, 1), (0, 3),
)


def dot(left, right, contract=((1,), (0,))):
    return lax.dot_general(left, right, (contract, ((), ())), preferred_element_type=F32)


def norm_rows(values):
    center = values - jnp.mean(values, axis=-1, keepdims=True)
    inverse = lax.rsqrt(jnp.mean(center * center, axis=-1, keepdims=True) + EPSILON)
    return center * inverse, inverse


def norm_back(grad_in, normed, inverse):
    grad_mean = jnp.mean(grad_in, axis=-1, keepdims=True)
    cross_mean = jnp.mean(grad_in * normed, axis=-1, keepdims=True)
    return inverse * (grad_in - grad_mean - normed * cross_mean)


def iota(shape, dim):
    return lax.broadcasted_iota(jnp.int32, shape, dim)


class Place:
    def __init__(self):
        self.r = lax.axis_index("rows")
        self.b = lax.axis_index("grp")
        self.x = self.r // 16
        self.z = (self.r // 4) % 4
        self.y = self.r % 4
        self.spot = self.x * 4 + self.y
        self.me = self.y * 4 + self.b
        self.flip = 2 * (self.z % 2)
        self.head = self.y * 4 + (self.b + self.flip) % 4
        toward = 2 * (self.b // 2) - 1
        self.near = (self.z + 4 + toward) % 4
        self.far = (self.z + 4 - toward) % 4
        self.opposite = (self.z + 2) % 4

    def mate(self, dy, c):
        y = (self.y + dy) % 4
        b = (self.b + 2 * (c // 2)) % 4
        if c % 2:
            b = b + 1 - 2 * (b % 2)
        head = y * 4 + (b + self.flip) % 4
        return y * 4 + b, head, (self.r - self.y + y, b)

    def link(self, b):
        return 2 * ((self.b // 2 + b // 2) % 2) + (self.b + b) % 2

    def same_head(self, z):
        return (self.r + (z - self.z) * 4, (self.b + 2) % 4)

    def plane(self, dx, dy):
        x, y = (self.x + dx) % 4, (self.y + dy) % 4
        return x * 4 + y, (self.r + (x - self.x) * 16 + (y - self.y), self.b)

    def along(self, axis, k):
        if axis == "x":
            place = (self.x + k) % 4
            return place, (self.r + (place - self.x) * 16, self.b)
        if axis == "z":
            place = (self.z + k) % 4
            return place, (self.r + (place - self.z) * 4, self.b)
        place = (self.y + k) % 4
        return place, (self.r + (place - self.y), self.b)

    def along_from(self, axis, k):
        return ({"x": self.x, "z": self.z, "y": self.y}[axis] + 4 - k) % 4


def remote(source, target, send, recv, device):
    return pltpu.make_async_remote_copy(
        src_ref=source,
        dst_ref=target,
        send_sem=send,
        recv_sem=recv,
        device_id=device,
        device_id_type=MESH,
    )


def total_of(ref, rows=slice(None)):
    value = ref[0, rows, :].astype(F32)
    for n in range(1, 4):
        value = value + ref[n, rows, :].astype(F32)
    return value


def pair_bias(pair, chain_cols, chain_all, chain_gain, w_pair_t, at, bias_send):
    cols = chain_cols[...]
    mine = cols[:, :BLOCK]
    for b in range(1, 4):
        mine = jnp.where(at.b == b, cols[:, b * BLOCK : (b + 1) * BLOCK], mine)
    head = iota((HEADS, 1), 0)
    gain = jnp.zeros((HEADS, 1), F32)
    for h in range(HEADS):
        gain = jnp.where(head == h, chain_gain[h], gain)
    strips = []
    for i in range(ROWS):
        normed, _ = norm_rows(pair[i].astype(F32))
        projected = dot(w_pair_t[...], normed.astype(BF16), ((1,), (1,)))
        same = (mine == chain_all[at.r * ROWS + i]).astype(F32)
        strips.append((projected + gain * same).astype(BF16))
    strips = jnp.concatenate(strips, axis=0)
    shape = (HEADS * 16, HEADS * ROWS)
    to, source = iota(shape, 0), iota(shape, 1)
    order = ((to // 16 == source % 16) & (to % 16 == source // 16)).astype(BF16)
    spread = dot(order, strips).astype(BF16)
    for h in range(HEADS):
        rows = spread[h * 16 : (h + 1) * 16]
        bias_send[h, :, :128] = rows[:, :128]
        bias_send[h, :, 128:] = jnp.concatenate([rows[:, 128:], jnp.zeros((16, 64), BF16)], axis=1)


def put_acts(part, first, second, acts_send):
    tail = jnp.concatenate([first[128:], second[128:]], axis=0)
    for n, piece in enumerate((first[:128], second[:128], tail)):
        piece = piece.T.astype(BF16)
        for h in range(HEADS):
            acts_send[h, part, n * HEAD : (n + 1) * HEAD, :] = piece[h * HEAD : (h + 1) * HEAD]


def assemble_bias(held):
    strips = []
    for y in range(4):
        parts = [held[y * 4 + b] for b in range(4)]
        tails = [p[:, 128:BLOCK] for p in parts]
        strips.append(jnp.concatenate([p[:, :128] for p in parts] + tails, axis=1))
    strips = jnp.concatenate(strips, axis=0)
    to, source = iota((HEAD, 64), 0), iota((HEAD, 64), 1)
    pick = ((source // 16 == to // ROWS) & (source % 16 == to % ROWS)).astype(BF16)
    return dot(pick, strips).astype(BF16)


def spread_bias(total, to_group):
    to, source = iota((64, HEAD), 0), iota((64, HEAD), 1)
    pick = ((to // 16 == source // ROWS) & (to % 16 == source % ROWS)).astype(BF16)
    spread = dot(pick, total).astype(BF16)
    for y in range(4):
        rows = spread[y * 16 : (y + 1) * 16]
        for b in range(4):
            tail = rows[:, 512 + b * 64 : 512 + (b + 1) * 64]
            to_group[y * 4 + b, :, :128] = rows[:, b * 128 : (b + 1) * 128]
            to_group[y * 4 + b, :, 128:] = jnp.concatenate([tail, jnp.zeros_like(tail)], axis=1)


def half(n):
    return slice(n * 64, n * 64 + 64)


def wide(acts, first, n):
    parts = [acts[first + b, 0, n * HEAD : (n + 1) * HEAD, :] for b in range(4)]
    parts += [acts[first + b, 0, 2 * HEAD :, half(n)] for b in range(4)]
    return jnp.concatenate(parts, axis=1)


def block(acts, place, n):
    return jnp.concatenate(
        [acts[place, 1, n * HEAD : (n + 1) * HEAD, :], acts[place, 1, 2 * HEAD :, half(n)]], axis=1
    )


def attend(query_t, grad_t, key_t, value_t, bias):
    scale = 1.0 / math.sqrt(HEAD)
    query = query_t.astype(F32).T.astype(BF16)
    grad = grad_t.astype(F32).T.astype(BF16)
    scores = dot(query, key_t) * (scale * LOG2E) + bias
    weight = jnp.exp2(scores)
    prob = weight * (1.0 / jnp.sum(weight, axis=-1, keepdims=True))
    grad_prob = dot(grad, value_t)
    scaled = prob * grad_prob
    grad_score = scaled - prob * jnp.sum(scaled, axis=-1, keepdims=True)
    return prob.astype(BF16), grad_score.astype(BF16), grad_score


def thin_rows(spread):
    shape = (16 * 16, BLOCK) if spread else (BLOCK, 16 * 16)
    thin, full = iota(shape, 0 if spread else 1), iota(shape, 1 if spread else 0)
    return ((thin // 16 == full // ROWS) & (thin % 16 == full % ROWS)).astype(BF16)


def back_pieces(grads, part):
    def piece(n):
        rows = [grads[h, part, n * HEAD : (n + 1) * HEAD, :] for h in range(HEADS)]
        return jnp.concatenate(rows, axis=0).astype(F32).T.astype(BF16)

    tail = piece(2)
    return [jnp.concatenate([piece(n), tail[n * 64 : n * 64 + 64]], axis=0) for n in (0, 1)]


def pair_weight(w_pair_t):
    shape = (HEADS * 16, HEADS)
    pick = (iota(shape, 0) // 16 == iota(shape, 1)).astype(BF16)
    return dot(pick, w_pair_t[...]).astype(BF16)


def pair_back(grad_t, weight, pair, result, rows):
    row = iota(weight.shape, 0) % 16
    for i in rows:
        grad = dot(grad_t, jnp.where(row == i, weight, jnp.zeros_like(weight)))
        normed, inverse = norm_rows(pair[i].astype(F32))
        result[i] = norm_back(grad, normed, inverse).astype(BF16)


def block_kernel(
    single_in, pair_in, noised_in, cotangent_in,
    w_gamma_in, w_beta_in, w_outgate_in, w_query_in, w_key_in, w_value_in, w_out_in,
    chain_in, cols_in, gain_in, w_pair_in,
    updated_out, plane_out, d_pair_out,
    single, pair, noised, cotangent, w_gamma, w_beta, w_outgate, w_query, w_key, w_value, w_out,
    bias_send, held, bias_all, acts_send, acts_all, gamma_v, gate_v, bias_f,
    key_t, value_t, grad_key, grad_value,
    to_x, from_x, to_z, from_z, to_group, from_group, grads_send, grads_all,
    part, plane_in, sum_z, own, updated, d_pair, sums_v, inner_v, chain_all, chain_cols, chain_gain, w_pair_t,
    load, sent, got, q_recv, x_recv, u_recv, z_recv,
):
    at = Place()
    barrier = pltpu.get_barrier_semaphore()
    others = [(dx, dy) for dx in (2, 1, 3, 0) for dy in (2, 1, 3, 0) if dx or dy]
    mates = [(dy, c) for dy in (1, 2, 3, 0) for c in (2, 3, 0, 1) if (dy, c) != (0, 0)]
    peers = (
        [at.along("z", k)[1] for k in (2, 1, 3)]
        + [at.same_head(at.far), at.same_head(at.near)]
        + [at.along("x", k)[1] for k in (2, 1, 3)]
        + [at.mate(dy, c)[2] for dy, c in mates]
        + [at.plane(dx, dy)[1] for dx, dy in others if dx and dy]
    )
    loads = {}
    for n, (name, source, target) in enumerate(
        (
            ("chain", chain_in, chain_all),
            ("gain", gain_in, chain_gain),
            ("cols", cols_in, chain_cols),
            ("map", w_pair_in, w_pair_t),
            ("pair", pair_in, pair),
            ("single", single_in, single),
            ("gamma", w_gamma_in, w_gamma),
            ("beta", w_beta_in, w_beta),
            ("noised", noised_in, noised),
            ("key", w_key_in, w_key),
            ("value", w_value_in, w_value),
            ("gate", w_outgate_in, w_outgate),
            ("cot", cotangent_in, cotangent),
            ("out", w_out_in, w_out),
            ("query", w_query_in, w_query),
        )
    ):
        loads[name] = pltpu.make_async_copy(source, target, load.at[n])
        loads[name].start()
        if name == "pair":
            for device in peers:
                pl.semaphore_signal(barrier, inc=1, device_id=device, device_id_type=MESH)

    def send(source, target, ssem, rsem, device):
        remote(source, target, ssem, rsem, device).start()

    def arrive(buffer, rsem):
        remote(buffer, buffer, sent.at[0], rsem, at.along("x", 1)[1]).wait_recv()

    def left(buffer, ssem):
        remote(buffer, buffer, ssem, got.at[0], at.along("x", 1)[1]).wait_send()

    bias_sent, kv_sent, q_sent, z_sent, x_sent, rows_sent, grads_sent = [sent.at[n] for n in range(7)]
    u_sent, near_sent, group_sent, plane_sent, sum_sent, out_sent = [sent.at[n] for n in range(7, 13)]
    bias_got, kv_got, rows_got, grads_got, group_got, plane_got, sum_got, out_got = [
        got.at[n] for n in range(8)
    ]

    for name in ("chain", "gain", "cols", "map", "pair"):
        loads[name].wait()
    pair_bias(pair, chain_cols, chain_all, chain_gain, w_pair_t, at, bias_send)
    pl.semaphore_wait(barrier, len(peers))
    for dy, c in mates:
        _, head, device = at.mate(dy, c)
        send(bias_send.at[head], held.at[at.me], bias_sent, bias_got, device)
    held[at.me] = bias_send[at.head]
    def send_kv(mates):
        for dy, c in mates:
            _, head, device = at.mate(dy, c)
            send(acts_send.at[head, 0], acts_all.at[at.me, 0], kv_sent, kv_got, device)

    for name in ("single", "gamma", "beta", "noised", "key", "value"):
        loads[name].wait()
    single_norm, _ = norm_rows(single[...].astype(F32))
    single_b = single_norm.astype(BF16)
    gamma = jax.nn.sigmoid(dot(single_b, w_gamma[...]))
    beta = dot(single_b, w_beta[...])
    gamma_v[...] = gamma
    noised_norm, _ = norm_rows(noised[...].astype(F32))
    x_b = (noised_norm * gamma + beta).astype(BF16)
    put_acts(0, dot(x_b, w_key[...]), dot(x_b, w_value[...]), acts_send)
    send_kv(MIXED[:8])
    for name in ("gate", "cot", "out", "query"):
        loads[name].wait()
    gate = jax.nn.sigmoid(dot(single_b, w_outgate[...]))
    gate_v[...] = gate
    grad_update = (cotangent[...].astype(F32) * gate).astype(BF16)
    grad_attn = dot(grad_update, w_out[...], ((1,), (1,)))
    put_acts(1, dot(x_b, w_query[...]), grad_attn, acts_send)
    acts_all[at.me] = acts_send[at.head]
    arrive(held.at[:15], bias_got)
    bias_all[at.x, at.z] = assemble_bias(held)
    order = (at.z, at.near, at.far, at.opposite)
    rows = bias_all.at[at.x, at.z]
    send(rows, rows, z_sent, z_recv.at[1], at.same_head(at.far))
    send(rows, rows, z_sent, z_recv.at[0], at.same_head(at.near))
    send_kv(MIXED[8:])
    for kz in range(4):
        rows = bias_all.at[at.x, order[kz]]
        if kz:
            arrive(rows, z_recv.at[kz - 1])
        if kz == 2:
            send(rows, rows, z_sent, z_recv.at[2], at.same_head(at.near))
        for k in (1, 3, 2):
            send(rows, rows, x_sent, x_recv.at[k], at.along("x", k)[1])
        if kz == 0:
            for dy, c in MIXED:
                _, head, device = at.mate(dy, c)
                source, target = acts_send.at[head, 1], acts_all.at[at.me, 1]
                send(source, target, q_sent, q_recv.at[dy * 4 + c], device)
    arrive(acts_all.at[:15, 0], kv_got)
    samples = [(at.y + 4 - dy) % 4 for dy in (1, 2, 3, 0)]
    for s, dy in enumerate((1, 2, 3, 0)):
        key_t[s] = wide(acts_all, samples[s] * 4, 0)
        value_t[s] = wide(acts_all, samples[s] * 4, 1)
        grad_key[s] = jnp.zeros((HEAD, TOKENS), F32)
        grad_value[s] = jnp.zeros((HEAD, TOKENS), F32)

    scale = 1.0 / math.sqrt(HEAD)

    def step_body(step, carry):
        k = step + step // 2 - 2 * (step // 3)
        place, device = at.along("x", k)
        c = at.link(place)

        @pl.when(step > 0)
        def _():
            arrive(bias_all.at[place], x_recv.at[4 - k])

        @pl.when(c > 0)
        def _():
            arrive(acts_all.at[at.y * 4 + place, 1], q_recv.at[c])

        for s, dy in enumerate((1, 2, 3)):
            arrive(acts_all.at[samples[s] * 4 + place, 1], q_recv.at[dy * 4 + c])
        for z in range(4):
            bias_f[z * HEAD : (z + 1) * HEAD, :] = bias_all[place, z].astype(F32) * LOG2E

        def weigh(s):
            slot = samples[s] * 4 + place
            query_t = block(acts_all, slot, 0)
            grad_t = block(acts_all, slot, 1)
            return (query_t, grad_t) + attend(query_t, grad_t, key_t[s], value_t[s], bias_f[...])

        ahead = weigh(0)
        total = ahead[4]
        for s, dy in enumerate((1, 2, 3, 0)):
            query_t, grad_t, prob_b, score_b, _ = ahead
            if s < 3:
                ahead = weigh(s + 1)
                total = total + ahead[4]
            slot = samples[s] * 4 + place
            attended = dot(value_t[s], prob_b, ((1,), (1,))).astype(BF16)
            grad_query = (dot(key_t[s], score_b, ((1,), (1,))) * scale).astype(BF16)
            grad_value[s] = grad_value[s] + dot(grad_t, prob_b)
            grad_key[s] = grad_key[s] + dot(query_t, score_b)
            grads_send[slot, 1, :HEAD, :] = attended[:, :128]
            grads_send[slot, 1, HEAD : 2 * HEAD, :] = grad_query[:, :128]
            grads_send[slot, 1, 2 * HEAD :, :64] = attended[:, 128:]
            grads_send[slot, 1, 2 * HEAD :, 64:] = grad_query[:, 128:]
        for z in range(4):
            to_x[k, z] = total[z * HEAD : (z + 1) * HEAD].astype(BF16)

        @pl.when(step > 0)
        def _():
            for kz in (3, 2, 1, 0):
                z = order[kz]
                send(to_x.at[k, z], from_x.at[at.x, z], u_sent, u_recv.at[kz], device)

        for s, dy in enumerate((1, 2, 3, 0)):
            slot = samples[s] * 4 + place
            copy = remote(
                grads_send.at[slot, 1],
                grads_all.at[at.head, 1],
                rows_sent,
                rows_got,
                (at.r - at.y + samples[s], place),
            )
            if dy:
                copy.start()
            else:
                pl.when(c > 0)(copy.start)
        return carry

    lax.fori_loop(0, 4, step_body, 0)
    for s, dy in enumerate((1, 2, 3, 0)):
        key_b = (grad_key[s] * scale).astype(BF16)
        value_b = grad_value[s].astype(BF16)
        for b in range(4):
            slot = samples[s] * 4 + b
            lanes = slice(b * 128, (b + 1) * 128)
            tail = slice(512 + b * 64, 512 + (b + 1) * 64)
            grads_send[slot, 0, :HEAD, :] = key_b[:, lanes]
            grads_send[slot, 0, HEAD : 2 * HEAD, :] = value_b[:, lanes]
            grads_send[slot, 0, 2 * HEAD :, :64] = key_b[:, tail]
            grads_send[slot, 0, 2 * HEAD :, 64:] = value_b[:, tail]
        for c in (2, 0, 3, 1):
            if dy or c:
                slot, _, device = at.mate(4 - dy, c)
                send(grads_send.at[slot, 0], grads_all.at[at.head, 0], grads_sent, grads_got, device)
    grads_all[at.head] = grads_send[at.me]
    from_x[at.x] = to_x[0]
    left(held.at[:15], bias_sent)
    left(acts_all.at[:15, 0], kv_sent)
    left(acts_all.at[:15, 1], q_sent)
    left(bias_all.at[0, :3], z_sent)
    left(bias_all.at[:3], x_sent)
    arrive(grads_all.at[:15, 1], rows_got)
    attended, grad_q = back_pieces(grads_all, 1)
    gamma = gamma_v[...]
    gate = gate_v[...]
    block_update = dot(attended, w_out[...])
    noised_f = noised[...].astype(F32)
    updated[...] = (noised_f + gate * block_update).astype(BF16)
    noised_norm, _ = norm_rows(noised_f)
    back = ((1,), (1,))
    pre_gate = (cotangent[...].astype(F32) * block_update * (gate * (1.0 - gate))).astype(BF16)
    sums_v[...] = dot(pre_gate, w_outgate[...], back)
    inner_v[...] = dot(grad_q, w_query[...], back)
    gamma_v[...] = noised_norm * (gamma * (1.0 - gamma))
    save = pltpu.make_async_copy(updated, updated_out, load.at[0])
    save.start()

    def rows_for(kz):
        z = order[kz]
        arrive(from_x.at[:3, z], u_recv.at[kz])
        rows = from_x[0, z].astype(F32)
        for x in range(1, 4):
            rows = rows + from_x[x, z].astype(F32)
        return rows

    to_z[3] = rows_for(3).astype(BF16)
    send(to_z.at[3], from_z.at[3], near_sent, z_recv.at[5], at.same_head(at.near))
    to_z[1] = rows_for(1).astype(BF16)
    send(to_z.at[1], from_z.at[1], near_sent, z_recv.at[3], at.same_head(at.near))
    arrive(grads_all.at[:15, 0], grads_got)
    grad_k, grad_v = back_pieces(grads_all, 0)
    grad_input = inner_v[...] + dot(grad_k, w_key[...], back) + dot(grad_v, w_value[...], back)
    pre_gamma = (grad_input * gamma_v[...]).astype(BF16)
    sums = sums_v[...] + dot(pre_gamma, w_gamma[...], back)
    sums = sums + dot(grad_input.astype(BF16), w_beta[...], back)
    spread = dot(thin_rows(True), sums.astype(BF16)).astype(BF16)
    for p in range(16):
        part[p] = spread[p * 16 : (p + 1) * 16]
    for dx, dy in others:
        place, device = at.plane(dx, dy)
        send(part.at[place], plane_in.at[at.spot], plane_sent, plane_got, device)
    plane_in[at.spot] = part[at.spot]

    to_far = rows_for(2)
    arrive(from_z.at[3], z_recv.at[5])
    to_z[2] = (to_far + from_z[3].astype(F32)).astype(BF16)
    send(to_z.at[2], from_z.at[2], near_sent, z_recv.at[4], at.same_head(at.far))
    left(grads_all.at[:15, 1], rows_sent)
    left(grads_all.at[:15, 0], grads_sent)
    left(from_x.at[:3], u_sent)
    own_rows = rows_for(0)
    weight = pair_weight(w_pair_t)
    shape = (16, BLOCK)
    mine = iota(shape, 0) + at.spot * ROWS
    pick = ((iota(shape, 1) == mine) & (iota(shape, 0) < ROWS)).astype(BF16)
    normed, inverse = norm_rows(dot(pick, single[...]))
    arrive(plane_in.at[:15], plane_got)
    total = plane_in[0].astype(F32)
    for p in range(1, 16):
        total = total + plane_in[p].astype(F32)
    sum_z[at.z] = total.astype(BF16)
    for k in (2, 1, 3):
        rows = sum_z.at[at.z]
        send(rows, rows, sum_sent, sum_got, at.along("z", k)[1])
    for kz in (1, 2):
        arrive(from_z.at[kz], z_recv.at[2 + kz])
    own_rows = own_rows + from_z[1].astype(F32) + from_z[2].astype(F32)
    spread_bias((own_rows * TOKENS).astype(BF16), to_group)
    for dy, c in mates:
        slot, _, device = at.mate(dy, c)
        send(to_group.at[slot], from_group.at[at.head], group_sent, group_got, device)
    from_group[at.head] = to_group[at.me]
    arrive(sum_z.at[:3], sum_got)
    own[...] = norm_back(total_of(sum_z), normed, inverse).astype(BF16)
    for dx, dy in others:
        send(own, plane_out.at[at.spot], out_sent, out_got, at.plane(dx, dy)[1])
    put = pltpu.make_async_copy(own, plane_out.at[at.spot], load.at[2])
    put.start()
    arrive(from_group.at[:15], group_got)
    grad_t = jnp.concatenate([from_group[h] for h in range(HEADS)], axis=0)
    grad_t = grad_t.astype(F32).T.astype(BF16)[:BLOCK]
    pair_back(grad_t, weight, pair, d_pair, range(ROWS))
    keep = pltpu.make_async_copy(d_pair, d_pair_out, load.at[1])
    keep.start()
    left(from_z.at[:3], near_sent)
    left(plane_in.at[:15], plane_sent)
    left(sum_z.at[:3], sum_sent)
    left(from_group.at[:15], group_sent)
    save.wait()
    keep.wait()
    put.wait()
    left(plane_in.at[:15], out_sent)
    arrive(plane_out.at[:15], out_got)


def finish_kernel(*refs):
    sources, results, held, sums, sems = refs[:3], refs[3:6], refs[6:9], refs[9], refs[10]
    loads = [pltpu.make_async_copy(sources[n], held[n], sems.at[n]) for n in range(3)]
    ready = (held[0], sums, held[2])
    stores = [pltpu.make_async_copy(ready[n], results[n], sems.at[3 + n]) for n in range(3)]
    for copy in loads:
        copy.start()
    pick = thin_rows(False)
    for n in range(3):
        loads[n].wait()
        if n == 1:
            sums[...] = dot(pick, jnp.concatenate([held[1][p] for p in range(16)], axis=0))
        stores[n].start()
    for copy in stores:
        copy.wait()


def on_device(
    single,
    pair,
    chains,
    noised,
    w_gamma,
    w_beta,
    w_outgate,
    w_query,
    w_key,
    w_value,
    w_out,
    w_pair,
    chain_gain,
    cotangent,
):
    def space(*shape):
        return pltpu.VMEM(shape, BF16)

    def wide_space(*shape):
        return pltpu.VMEM(shape, F32)

    def dma(count):
        return pltpu.SemaphoreType.DMA((count,))

    half_width = WIDTH // 2
    results = pl.pallas_call(
        block_kernel,
        out_shape=[
            jax.ShapeDtypeStruct((BLOCK, WIDTH), BF16),
            jax.ShapeDtypeStruct((16, 16, half_width), BF16),
            jax.ShapeDtypeStruct(pair.shape, BF16),
        ],
        in_specs=[ANY] * 15,
        out_specs=[ANY] * 3,
        scratch_shapes=[
            space(BLOCK, half_width),
            space(ROWS, BLOCK, 128),
            space(BLOCK, WIDTH),
            space(BLOCK, WIDTH),
        ]
        + [space(half_width, WIDTH)] * 3
        + [space(WIDTH, WIDTH)] * 4
        + [
            space(16, 16, 256),
            space(16, 16, 256),
            space(4, 4, HEAD, TOKENS),
            space(16, 2, CHUNK, 128),
            space(16, 2, CHUNK, 128),
            wide_space(BLOCK, WIDTH),
            wide_space(BLOCK, WIDTH),
            wide_space(BLOCK, TOKENS),
            space(4, HEAD, TOKENS),
            space(4, HEAD, TOKENS),
            wide_space(4, HEAD, TOKENS),
            wide_space(4, HEAD, TOKENS),
            space(4, 4, HEAD, TOKENS),
            space(4, 4, HEAD, TOKENS),
            space(4, HEAD, TOKENS),
            space(4, HEAD, TOKENS),
            space(16, 16, 256),
            space(16, 16, 256),
            space(16, 2, CHUNK, 128),
            space(16, 2, CHUNK, 128),
        ]
        + [
            space(16, 16, half_width),
            space(16, 16, half_width),
            space(4, 16, half_width),
            space(16, half_width),
        ]
        + [space(BLOCK, WIDTH), space(ROWS, BLOCK, 128)]
        + [wide_space(BLOCK, half_width), wide_space(BLOCK, WIDTH)]
        + [
            pltpu.SMEM((TOKENS,), jnp.int32),
            pltpu.VMEM((1, TOKENS), jnp.int32),
            pltpu.SMEM((HEADS,), F32),
            space(HEADS, 128),
        ]
        + [dma(15), dma(13), dma(8), dma(16), dma(4), dma(4), dma(6)],
        compiler_params=pltpu.CompilerParams(
            vmem_limit_bytes=VMEM_BYTES, collective_id=0, has_side_effects=True
        ),
        name="block",
    )(
        single,
        pair,
        noised.reshape(BLOCK, WIDTH),
        cotangent.reshape(BLOCK, WIDTH),
        w_gamma,
        w_beta,
        w_outgate,
        w_query,
        w_key,
        w_value,
        w_out,
        chains,
        chains.reshape(1, TOKENS),
        chain_gain,
        w_pair.T,
    )
    updated, d_single, d_pair = pl.pallas_call(
        finish_kernel,
        out_shape=[
            jax.ShapeDtypeStruct((BLOCK, WIDTH), BF16),
            jax.ShapeDtypeStruct((BLOCK, half_width), F32),
            jax.ShapeDtypeStruct(pair.shape, BF16),
        ],
        in_specs=[ANY] * 3,
        out_specs=[ANY] * 3,
        scratch_shapes=[
            space(BLOCK, WIDTH),
            space(16, 16, half_width),
            space(*pair.shape),
            wide_space(BLOCK, half_width),
            dma(6),
        ],
        compiler_params=pltpu.CompilerParams(vmem_limit_bytes=VMEM_BYTES),
        name="finish",
    )(*results)
    return updated.reshape(1, BLOCK, WIDTH), d_single, d_pair


def solution(mesh):
    rows = P("rows", "grp", None)
    grp = P("grp", None)
    in_specs = (grp, rows, P(), rows) + (P(),) * 9 + (rows,)
    return jax.shard_map(
        on_device, mesh=mesh, in_specs=in_specs, out_specs=(rows, grp, rows), check_vma=False
    )
```
